512 devices in a mesh: dp: 2 (over core), ctx: 32 (over z_hi, y), tp: 8 (over z_lo, x).
Axes of the slice: x: 4, y: 8, z: 8 (z_hi: 4, z_lo: 2; z = z_hi * 2 + z_lo), core: 2. Of those that a mesh axis runs over, the one named last changes fastest.
Arguments:
- q_in: bfloat16 [2, 4096, 5120], P('dp', 'ctx', 'tp'), may hold values from -10 to 10
- key_input: bfloat16 [2, 4096, 1024], P('dp', 'ctx', 'tp'), may hold values from -10 to 10
- value_input: bfloat16 [2, 4096, 1024], P('dp', 'ctx', 'tp'), may hold values from -6 to 6
- q_bias: float32 [5120], P('tp'), may hold values from -3 to 3
- key_bias: float32 [1024], P('tp'), may hold values from -3 to 3
- value_bias: float32 [1024], P('tp'), may hold values from -3 to 3
- out_weight: bfloat16 [5120, 5120], P('tp', 'dp'), may hold values from -0.078125 to 0.078125
- out_grad: bfloat16 [2, 4096, 5120], P('dp', ('ctx', 'tp')), may hold values from -5 to 5
- doc_lengths: int32 [2, 8], P('dp'), may hold values from 1 to 2048, 4096 in all within a row
- block_pos: int32 [2, 32, 2], P('dp'), may hold values from 0 to 63, as said below
Outputs:
- out: bfloat16 [2, 4096, 5120], P('dp', ('ctx', 'tp'))
- q_grad: bfloat16 [2, 4096, 5120], P('dp', 'ctx', 'tp')
- k_grad: bfloat16 [2, 4096, 1024], P('dp', 'ctx', 'tp')
- v_grad: bfloat16 [2, 4096, 1024], P('dp', 'ctx', 'tp')
- q_bias_grad: float32 [5120], P('tp')
- k_bias_grad: float32 [1024], P('tp')
- v_bias_grad: float32 [1024], P('tp')
The draws below stay inside these ranges and needn't reach their ends.
Inputs may be any that keep to these rules, and one draw needn't show every extreme that they name: `block_pos`: for each sequence, the first entries over the indices of ctx are a permutation of 0 to 31, and each second entry is 63 minus the first entry beside it.
All inputs are finite; a program needn't handle non-finite values.
Results may differ from the reference program's by a relative error of at most 0.04.
Values may be sent and summed in bfloat16 or wider, within the bound.
A program may use at most 64 MiB of HBM per device.

```python
import math
import jax
import jax.numpy as jnp
import numpy as np
from jax import lax

D = 5120
HQ = 40
KEY_HEADS = 8
HEAD_WIDTH = 128
QUERY_PER_KEY = 5
QUERY_FEATURES = 5120
KW = 1024
STORED_ROWS = 128
BLK = 64
BLOCKS = 64
SEQUENCE_TOKENS = 4096
SEQUENCE_COUNT = 2
NDOCS = 8
MOSTDOC = 2048
N_CTX = 32
N_TP = 8


def draw_q_in(key, part):
    key = jax.random.fold_in(key, 1)
    entries = jax.random.normal(key, (SEQUENCE_COUNT, SEQUENCE_TOKENS, QUERY_FEATURES), jnp.float32)
    return jnp.clip(entries, -10.0, 10.0).astype(jnp.bfloat16)


def draw_key_input(key, part):
    key = jax.random.fold_in(key, 4)
    entries = jax.random.normal(key, (SEQUENCE_COUNT, SEQUENCE_TOKENS, KW), jnp.float32)
    return jnp.clip(entries, -10.0, 10.0).astype(jnp.bfloat16)


def draw_block_pos(key, part):
    key = jax.random.fold_in(key, 7)
    seq_keys = jax.random.split(key, SEQUENCE_COUNT)
    lighter = jax.vmap(lambda single: jax.random.permutation(single, BLOCKS // 2))(seq_keys).astype(jnp.int32)
    return jnp.stack([lighter, BLOCKS - 1 - lighter], axis=2)


def block_scale(key, dims, pieces, least, largest):
    level, own = 1.0, jax.random.fold_in(key, 6)
    for dim, parts in pieces:
        draws = jnp.exp(jax.random.uniform(jax.random.fold_in(own, dim), (parts,), jnp.float32, least / len(pieces), largest / len(pieces)))
        level = level * jnp.repeat(draws, dims[dim] // parts).reshape([-1 if axis == dim else 1 for axis in range(len(dims))])
    return level


def split_up(number_of, total, most, skew):
    weights = [(1 << 20) // math.isqrt(rank ** skew) + 1 for rank in range(2, number_of + 1)]
    spare, holding = total - most - (number_of - 1), [1] * (number_of - 1)
    while spare > 0:
        free = [i for i in range(number_of - 1) if holding[i] < most]
        pool, left = sum([weights[i] for i in free]), spare
        for i in free:
            addition = min(most - holding[i], max(1, left * weights[i] // pool), spare)
            holding[i] = holding[i] + addition
            spare = spare - addition
    return np.array([most] + holding)


def uneven_parts(stream_key, amount, total, most, lean):
    if amount == 2:
        one = jax.random.randint(stream_key, (), max(1, total - most), min(most, total - 1) + 1)
        return jnp.stack([one, total - one])
    sizes = jnp.asarray(split_up(amount, total, most, lean), jnp.int32)
    twos = (amount - 1) // 2
    donor, taker = sizes[1:1 + 2 * twos:2], sizes[2:2 + 2 * twos:2]
    room = jnp.minimum(donor - 1, most - taker)
    passed = jax.random.randint(jax.random.fold_in(stream_key, 1), (twos,), 0, 1 << 20) % (room + 1)
    sizes = sizes.at[1:1 + 2 * twos:2].set(donor - passed).at[2:2 + 2 * twos:2].set(taker + passed)
    return sizes[jax.random.permutation(jax.random.fold_in(stream_key, 2), amount)]


def scatter_about(stream_key, dims, width, most, pieces=(), kind=jnp.bfloat16):
    loudness = block_scale(stream_key, dims, pieces, -0.22, 0.18) if pieces else 1.0
    values = jax.random.normal(stream_key, dims, jnp.float32) * width * loudness
    return jnp.minimum(jnp.maximum(values, -most), most).astype(kind)


def setup_inputs(seed: int = 0) -> dict:
    streams_of = jax.random.split(jax.random.key(seed), 11)
    q_in = draw_q_in(jax.random.fold_in(streams_of[10], 71), 0)
    key_input = draw_key_input(jax.random.fold_in(streams_of[10], 71), 0)
    value_input = scatter_about(streams_of[2], (SEQUENCE_COUNT, SEQUENCE_TOKENS, KW), 1.0, 6.0, ((0, 2), (1, 32), (2, 8)))
    q_bias = scatter_about(streams_of[3], (QUERY_FEATURES,), 0.5, 3.0, ((0, 8),), jnp.float32)
    key_bias = scatter_about(streams_of[4], (KW,), 0.5, 3.0, ((0, 8),), jnp.float32)
    value_bias = scatter_about(streams_of[5], (KW,), 0.5, 3.0, ((0, 8),), jnp.float32)
    out_weight = scatter_about(streams_of[6], (QUERY_FEATURES, D), QUERY_FEATURES ** -0.5, 0.078125, ((0, 8), (1, 2)))
    out_grad = scatter_about(streams_of[7], (SEQUENCE_COUNT, SEQUENCE_TOKENS, D), 0.35, 5.0, ((0, 2), (1, 256)))
    doc_lengths = jax.vmap(lambda own: uneven_parts(own, NDOCS, SEQUENCE_TOKENS, MOSTDOC, 2))(jax.random.split(streams_of[8], SEQUENCE_COUNT)).reshape((SEQUENCE_COUNT, NDOCS)).astype(jnp.int32)
    block_pos = draw_block_pos(jax.random.fold_in(streams_of[10], 71), 0)
    return dict(q_in=q_in, key_input=key_input, value_input=value_input, q_bias=q_bias, key_bias=key_bias, value_bias=value_bias, out_weight=out_weight, out_grad=out_grad, doc_lengths=doc_lengths, block_pos=block_pos)


ROPE_BASE = 1000000.0


def positions(blocks, block_width):
    offsets = jnp.arange(block_width, dtype=jnp.int32)
    starts = blocks.astype(jnp.int32)[:, :, None] * block_width
    return (starts + offsets[None, None, :]).reshape(-1)


def documents(lengths, token_pos):
    doc_ends = jnp.cumsum(lengths.astype(jnp.int32))
    return jnp.sum((doc_ends[None, :] <= token_pos[:, None]).astype(jnp.int32), axis=1)


def rotary(token_pos, head_size):
    frequency = ROPE_BASE ** (-jnp.arange(0, head_size, 2).astype(jnp.float32) / head_size)
    phases = token_pos.astype(jnp.float32)[:, None] * frequency[None, :]
    phases = jnp.concatenate([phases, phases], axis=1)
    return jnp.cos(phases)[:, None, :], jnp.sin(phases)[:, None, :]


def apply_rotary(field, cosine_values, sine_values):
    half_width = field.shape[-1] // 2
    turned = jnp.concatenate([-field[..., half_width:], field[..., :half_width]], axis=-1)
    return field * cosine_values + turned * sine_values


def roundtrip(field):
    return lax.optimization_barrier(field.astype(jnp.bfloat16)).astype(jnp.float32)


def reference(q_in, key_input, value_input, q_bias, key_bias, value_bias, out_weight, out_grad, doc_lengths, block_pos):
    score_scale = HEAD_WIDTH ** -0.5
    head_cols = QUERY_FEATURES // N_TP
    outputs, query_grads, key_grads, value_grads = [], [], [], []
    query_bias_sum = jnp.zeros((QUERY_FEATURES,), jnp.float32)
    key_bias_sum = jnp.zeros((KW,), jnp.float32)
    value_bias_sum = jnp.zeros((KW,), jnp.float32)
    for sequence_index in range(SEQUENCE_COUNT):
        token_pos = positions(block_pos[sequence_index], BLK)
        token_doc = documents(doc_lengths[sequence_index], token_pos)
        cosine_values, sine_values = rotary(token_pos, HEAD_WIDTH)
        query = apply_rotary(q_in[sequence_index].astype(jnp.float32).reshape(SEQUENCE_TOKENS, HQ, HEAD_WIDTH) + q_bias.reshape(HQ, HEAD_WIDTH), cosine_values, sine_values).astype(jnp.bfloat16)
        key_row_block = apply_rotary(key_input[sequence_index].astype(jnp.float32).reshape(SEQUENCE_TOKENS, KEY_HEADS, HEAD_WIDTH) + key_bias.reshape(KEY_HEADS, HEAD_WIDTH), cosine_values, sine_values).astype(jnp.bfloat16)
        value_row_block = (value_input[sequence_index].astype(jnp.float32) + value_bias).astype(jnp.bfloat16).reshape(SEQUENCE_TOKENS, KEY_HEADS, HEAD_WIDTH)
        key_wide = key_row_block.astype(jnp.float32)
        value_wide = value_row_block.astype(jnp.float32)

        def per_shard(accumulated, inputs):
            key_acc, value_acc = accumulated
            query_row_block, query_pos, query_doc, grad_rows = inputs
            grouped_heads = query_row_block.astype(jnp.float32).reshape(STORED_ROWS, KEY_HEADS, QUERY_PER_KEY, HEAD_WIDTH)
            scores = jnp.einsum("rkgd,lkd->kgrl", grouped_heads, key_wide) * score_scale
            allowed = (token_pos[None, :] <= query_pos[:, None]) & (token_doc[None, :] == query_doc[:, None])
            scores = jnp.where(allowed[None, None], scores, -jnp.inf)
            row_max = jnp.max(scores, axis=3, keepdims=True)
            row_sum = jnp.sum(jnp.exp(scores - row_max), axis=3, keepdims=True)
            log_total = row_max + jnp.log(row_sum)
            probability = roundtrip(jnp.exp(scores - log_total))
            attended_output = jnp.einsum("kgrl,lkd->rkgd", probability, value_wide).astype(jnp.bfloat16).reshape(STORED_ROWS, QUERY_FEATURES)
            mixed_rows = jnp.zeros((STORED_ROWS, D), jnp.float32)
            for tp_index in range(N_TP):
                low = tp_index * head_cols
                partial_rows = jnp.dot(attended_output[:, low:low + head_cols], out_weight[low:low + head_cols], preferred_element_type=jnp.float32)
                mixed_rows = mixed_rows + roundtrip(partial_rows)
            out_rows = mixed_rows.astype(jnp.bfloat16)
            attended_gradient = jnp.dot(grad_rows, out_weight.T, preferred_element_type=jnp.float32).astype(jnp.bfloat16)
            widened_gradient = attended_gradient.astype(jnp.float32).reshape(STORED_ROWS, KEY_HEADS, QUERY_PER_KEY, HEAD_WIDTH)
            grad_prob = jnp.einsum("rkgd,lkd->kgrl", widened_gradient, value_wide)
            row_correction = jnp.sum(widened_gradient * attended_output.astype(jnp.float32).reshape(STORED_ROWS, KEY_HEADS, QUERY_PER_KEY, HEAD_WIDTH), axis=3)
            row_correction = jnp.transpose(row_correction, (1, 2, 0))[..., None]
            grad_score = roundtrip(probability * (grad_prob - row_correction))
            grad_query = jnp.einsum("kgrl,lkd->rkgd", grad_score, key_wide) * score_scale
            key_term = roundtrip(jnp.einsum("kgrl,rkgd->lkd", grad_score, grouped_heads) * score_scale)
            value_term = roundtrip(jnp.einsum("kgrl,rkgd->lkd", probability, widened_gradient))
            return (key_acc + key_term, value_acc + value_term), (out_rows, grad_query.reshape(STORED_ROWS, HQ, HEAD_WIDTH))

        empty_gradient = jnp.zeros((SEQUENCE_TOKENS, KEY_HEADS, HEAD_WIDTH), jnp.float32)
        shards_in = (query.reshape(N_CTX, STORED_ROWS, HQ, HEAD_WIDTH), token_pos.reshape(N_CTX, STORED_ROWS), token_doc.reshape(N_CTX, STORED_ROWS), out_grad[sequence_index].reshape(N_CTX, STORED_ROWS, D))
        (key_acc, value_acc), (out_rows, grad_query) = lax.scan(per_shard, (empty_gradient, empty_gradient), shards_in)
        pre_query = apply_rotary(grad_query.reshape(SEQUENCE_TOKENS, HQ, HEAD_WIDTH), cosine_values, -sine_values).reshape(SEQUENCE_TOKENS, QUERY_FEATURES)
        pre_key = apply_rotary(key_acc, cosine_values, -sine_values).reshape(SEQUENCE_TOKENS, KW)
        grad_value = value_acc.reshape(SEQUENCE_TOKENS, KW)
        outputs.append(out_rows.reshape(SEQUENCE_TOKENS, D))
        query_grads.append(pre_query.astype(jnp.bfloat16))
        key_grads.append(pre_key.astype(jnp.bfloat16))
        value_grads.append(grad_value.astype(jnp.bfloat16))
        query_bias_sum = query_bias_sum + jnp.sum(pre_query, axis=0)
        key_bias_sum = key_bias_sum + jnp.sum(pre_key, axis=0)
        value_bias_sum = value_bias_sum + jnp.sum(grad_value, axis=0)
    return (jnp.stack(outputs), jnp.stack(query_grads), jnp.stack(key_grads), jnp.stack(value_grads), query_bias_sum, key_bias_sum, value_bias_sum)
```

```python
import functools

import jax
import jax.numpy as jnp
import numpy as np
from jax import lax
from jax.experimental import pallas as pl
from jax.experimental.pallas import tpu as pltpu
from jax.sharding import PartitionSpec as P

HW = 128
HALF = HW // 2
BLK = 64
ROPE_BASE = 1000000.0
NZ = 4
NZL = 2
CHUNK = 512
LOW = -1e30
LOG2E = 1.4426950408889634
MESH = pl.DeviceIdType.MESH
F32 = jnp.float32
BF16 = jnp.bfloat16
NT = (((1,), (1,)), ((), ()))
TN = (((0,), (0,)), ((), ()))


def dot(a, b):
    return jnp.dot(a, b, preferred_element_type=F32)


def turn(x):
    return pltpu.roll(x, HALF, 1)


class Wires:
    def __init__(self, send, recv):
        self.send, self.recv, self.all = send, recv, []

    def start(self, src, dst, target):
        n = len(self.all)
        copy = pltpu.make_async_remote_copy(
            src_ref=src,
            dst_ref=dst,
            send_sem=self.send.at[n],
            recv_sem=self.recv.at[n],
            device_id=target,
            device_id_type=MESH,
        )
        copy.start()
        self.all.append(copy)
        return copy

    def finish(self):
        for copy in self.all:
            copy.wait_send()


def kernel(
    dims,
    q_ref, k_ref, v_ref, qb_ref, kbias_ref, vbias_ref, freq_ref, bp_ref, doc_ref, w_hbm, og_hbm,
    out_ref, qg_ref, kg_ref, vg_ref, bias_ref,
    qn, qt, kb, vb, sb, eb, wb, og, dot_t, dot_n, o_rows, acc_o, acc_q, acc_g,
    pk, pv, rk_half, rk_full, rk_z, rv_half, rv_full, rv_z,
    po, rx_half, rx_full, rz, zs, mb, lb, ub, bpv, vs, btile, b_dp, b_z, b_y,
    local_sem, send_sem, recv_sem,
):
    NY, NX, G = dims
    ctx, tp, dp = lax.axis_index("ctx"), lax.axis_index("tp"), lax.axis_index("dp")
    z, y = ctx // NY, lax.rem(ctx, NY)
    zl, x = tp // NX, lax.rem(tp, NX)
    HY, HX = NY // 2, NX // 2
    QN = G * HW
    SUBS = NZ // 2
    ROWS = 4 * BLK

    def y_peer(d):
        return {"ctx": z * NY + lax.rem(y + d + NY, NY)}

    def z_peer(d):
        return {"ctx": lax.rem(z + d, NZ) * NY + y}

    def x_peer(d):
        return {"tp": zl * NX + lax.rem(x + d + NX, NX)}

    zl_peer = {"tp": (1 - zl) * NX + x}
    dp_peer = {"dp": 1 - dp}

    barrier = pltpu.get_barrier_semaphore()
    peers = [y_peer(d) for d in range(1, NY)] + [z_peer(d) for d in range(1, NZ)]
    peers += [x_peer(1), x_peer(-1), zl_peer, dp_peer]
    for peer in peers:
        pl.semaphore_signal(barrier, inc=1, device_id=peer, device_id_type=MESH)

    own_w = pltpu.make_async_copy(w_hbm, wb.at[dp], local_sem.at[0])
    own_w.start()
    own_g = pltpu.make_async_copy(og_hbm, og.at[tp], local_sem.at[1])
    own_g.start()

    b0, b1 = bp_ref[0, ctx, 0] * BLK, bp_ref[0, ctx, 1] * BLK
    sub = lax.broadcasted_iota(jnp.int32, (HW, HW), 0)
    pos = jnp.where(sub < BLK, b0 + sub, b1 + (sub - BLK))
    freq = freq_ref[...]
    angle = pos.astype(F32) * freq
    sign = jnp.where(lax.broadcasted_iota(jnp.int32, (1, HW), 1) < HALF, -1.0, 1.0)
    cos, sin = jnp.cos(angle), jnp.sin(angle) * sign
    inner = lax.broadcasted_iota(jnp.int32, (BLK, HW), 0).astype(F32) * freq
    cos_i, sin_i = jnp.cos(inner), jnp.sin(inner) * sign

    xk = k_ref[0].astype(F32) + kbias_ref[...]
    kb[0, 0] = (xk * cos + turn(xk) * sin).astype(BF16)
    vb[0, 0] = (v_ref[0].astype(F32) + vbias_ref[...]).astype(BF16)

    pl.semaphore_wait(barrier, len(peers))
    wires = Wires(send_sem, recv_sem)

    k_z = [wires.start(kb.at[0, 0], kb.at[0, r], z_peer(NZ - r)) for r in range(1, NZ)]
    g_x = [wires.start(og_hbm, og.at[tp], x_peer(d)) for d in (1, -1)]
    g_z = wires.start(og_hbm, og.at[tp], zl_peer)
    v_z = [wires.start(vb.at[0, 0], vb.at[0, r], z_peer(NZ - r)) for r in range(1, NZ)]
    far_w = wires.start(w_hbm, wb.at[dp], dp_peer)

    def gather_step(buf, k):
        if k < HY:
            up = wires.start(buf.at[(NY - (k - 1)) % NY], buf.at[NY - k], y_peer(1))
            down = wires.start(buf.at[k - 1], buf.at[k], y_peer(-1))
        else:
            lower, upper = pl.ds(0, NZ // 2), pl.ds(NZ // 2, NZ // 2)
            up = wires.start(buf.at[NY - k + 1, lower], buf.at[k, lower], y_peer(1))
            down = wires.start(buf.at[k - 1, upper], buf.at[k, upper], y_peer(-1))
        return [up, down]

    def arrived(copies):
        for copy in copies:
            copy.wait_recv()

    for h in range(G):
        cols = slice(h * HW, (h + 1) * HW)
        xq = q_ref[0, :, cols].astype(F32) + qb_ref[:, cols]
        rq = xq * cos + turn(xq) * sin
        qn[cols, :] = rq.astype(BF16)
        qt[:, cols] = rq.T.astype(BF16)
    lane = lax.broadcasted_iota(jnp.int32, (1, HW), 1)
    row_pos = jnp.where(lane < BLK, b0 + lane, b1 + (lane - BLK))
    end = jnp.int32(0)
    row_start = jnp.zeros((1, HW), jnp.int32)
    for d in range(doc_ref.shape[1]):
        row_start = jnp.where(row_pos >= end, end, row_start)
        end = end + doc_ref[0, d]
    row_pos = jnp.concatenate([row_pos] * G, axis=1)
    row_start = jnp.concatenate([row_start] * G, axis=1)
    mb[...] = jnp.full(mb.shape, LOW, F32)
    lb[...] = jnp.zeros(lb.shape, F32)
    vs[...] = jnp.zeros(vs.shape, F32)
    acc_o[...] = jnp.zeros(acc_o.shape, F32)
    acc_q[...] = jnp.zeros(acc_q.shape, F32)
    acc_g[...] = jnp.zeros(acc_g.shape, F32)

    def block_row(c, r):
        return lax.rem(z + r, NZ) * NY + lax.rem(y + c, NY)

    def base_step(i, carry):
        for h in range(2):
            bpv[pl.ds(2 * i + h, 1), :] = jnp.full((1, HW), bp_ref[0, i, h] * BLK, jnp.int32)
        return carry

    lax.fori_loop(0, NZ * NY, base_step, 0)

    def over(chunks, body):
        def step(i, carry):
            if len(chunks) == 1:
                c = chunks[0]
            else:
                c = chunks[0] + (i // SUBS) * (chunks[1] - chunks[0])
            body(c, lax.rem(i, SUBS))
            return carry

        lax.fori_loop(0, len(chunks) * SUBS, step, 0)

    def part_of(ref, c, p):
        return ref[c, pl.ds(2 * p, 2)].reshape(ROWS, HW)

    def score(c, p):
        s = dot(part_of(kb, c, p), qt[...])
        spot = lax.broadcasted_iota(jnp.int32, (BLK, QN), 0)
        most = mb[...]
        for j in range(4):
            base = bp_ref[0, block_row(c, 2 * p + j // 2), j % 2] * BLK
            piece = s[j * BLK:(j + 1) * BLK]
            piece = jnp.where((spot <= row_pos - base) & (spot >= row_start - base), piece, LOW)
            sb[c, p, j * BLK:(j + 1) * BLK, :] = piece
            most = jnp.maximum(most, jnp.max(piece.reshape(BLK // 8, 8, QN), axis=0))
        mb[...] = most

    def chunks_at(k):
        return [0] if k == 0 else [HY] if k == HY else [k, NY - k]

    arrived(k_z)
    k_y = {1: gather_step(kb, 1)}
    v_y = {}
    over(chunks_at(0), score)
    arrived(v_z)

    w_cols = wb.shape[2]
    left, right = pl.ds(0, w_cols), pl.ds(w_cols, w_cols)
    g_half = []
    g_next, g_last = [], []

    def opposite(line):
        from_left = zl_line(line) + lax.rem(x + NX - 1, NX)
        from_right = zl_line(line) + lax.rem(x + 1, NX)
        return [
            wires.start(og.at[from_left, :, left], og.at[from_left, :, left], x_peer(1)),
            wires.start(og.at[from_right, :, right], og.at[from_right, :, right], x_peer(-1)),
        ]

    def zl_line(line):
        return (zl if line == 0 else 1 - zl) * NX

    for k in range(1, HY):
        arrived(k_y[k])
        k_y[k + 1] = gather_step(kb, k + 1)
        if k > 1:
            arrived(v_y[k - 1])
        v_y[k] = gather_step(vb, k)
        if k == 1:
            arrived(g_x)
            g_half = opposite(0)
            g_z.wait_recv()
            partner = zl_line(1) + x
            g_next = [wires.start(og.at[partner], og.at[partner], x_peer(d)) for d in (1, -1)]
        over(chunks_at(k), score)
        if k == HY - 1:
            arrived(g_next)
            g_last = opposite(1)

    own_g.wait()
    own_w.wait()
    arrived(g_half)
    arrived(g_last)
    n_inner = w_cols // CHUNK

    def project(half):
        def step(n, carry):
            w = wb[half, :, pl.ds(pl.multiple_of(n * CHUNK, CHUNK), CHUNK)]
            at = pl.multiple_of(half * w_cols + n * CHUNK, CHUNK)
            g = og[:, :, pl.ds(at, CHUNK)].reshape(HW, CHUNK)
            acc_g[...] += lax.dot_general(w, g, NT, preferred_element_type=F32)
            return carry

        lax.fori_loop(0, n_inner, step, 0)

    project(dp)
    arrived(v_y[HY - 1])
    v_y[HY] = gather_step(vb, HY)
    far_w.wait_recv()
    project(1 - dp)
    for h in range(G):
        dot_t[:, h * HW:(h + 1) * HW] = acc_g[h * HW:(h + 1) * HW, :].astype(BF16)

    arrived(k_y[HY])
    over(chunks_at(HY), score)

    scale = HW ** -0.5
    top = jnp.max(mb[...], axis=0, keepdims=True) * (scale * LOG2E)

    def soften(i, carry):
        c, p = i // SUBS, lax.rem(i, SUBS)
        total = lb[...]
        for j in range(4):
            rows = slice(j * BLK, (j + 1) * BLK)
            e = jnp.exp2(sb[c, p, rows, :] * (scale * LOG2E) - top)
            total = total + jnp.sum(e.reshape(BLK // 8, 8, QN), axis=0)
            eb[c, p, rows, :] = e.astype(BF16)
        lb[...] = total
        return carry

    lax.fori_loop(0, NY * SUBS, soften, 0)
    inv = 1.0 / jnp.sum(lb[...], axis=0, keepdims=True)
    for h in range(G):
        cols = slice(h * HW, (h + 1) * HW)
        scaled = dot_t[:, cols].astype(F32) * inv[:, cols]
        dot_n[cols, :] = scaled.T.astype(BF16)

    def value_grad(c, p):
        g = dot(eb[c, p], dot_n[...])
        vs[...] += jnp.sum(g.reshape(ROWS // 8, 8, HW), axis=0)
        pv[c, pl.ds(2 * p, 2)] = g.astype(BF16).reshape(2, HW, HW)

    def attend(i, carry):
        c, p = i // SUBS, lax.rem(i, SUBS)
        acc_o[...] += lax.dot_general(part_of(vb, c, p), eb[c, p], TN, preferred_element_type=F32)
        return carry

    def scatter_step(buf, half, full, k):
        if k == 0:
            lower, upper = pl.ds(0, NZ // 2), pl.ds(NZ // 2, NZ // 2)
            up = wires.start(buf.at[HY, lower], half.at[0], y_peer(1))
            down = wires.start(buf.at[HY, upper], half.at[1], y_peer(-1))
        else:
            up = wires.start(buf.at[HY - k], full.at[k - 1, 0], y_peer(1))
            down = wires.start(buf.at[HY + k], full.at[k - 1, 1], y_peer(-1))
        return [up, down]

    def take(buf, half, full, k, copies):
        arrived(copies)
        if k == 0:
            for c, rows, i in ((HY - 1, slice(0, NZ // 2), 0), (HY + 1, slice(NZ // 2, NZ), 1)):
                buf[c, rows] = (buf[c, rows].astype(F32) + half[i].astype(F32)).astype(BF16)
        elif k < HY - 1:
            for c, i in ((HY - 1 - k, 0), (HY + 1 + k, 1)):
                buf[c] = (buf[c].astype(F32) + full[k - 1, i].astype(F32)).astype(BF16)
        else:
            both = full[k - 1, 0].astype(F32) + full[k - 1, 1].astype(F32)
            buf[0] = (buf[0].astype(F32) + both).astype(BF16)

    v_bufs, k_bufs = (pv, rv_half, rv_full), (pk, rk_half, rk_full)

    over(chunks_at(HY), value_grad)
    v_r = scatter_step(*v_bufs, 0)
    over(chunks_at(HY - 1), value_grad)
    arrived(v_y[HY])
    take(*v_bufs, 0, v_r)
    v_r = scatter_step(*v_bufs, 1)
    lax.fori_loop(0, NY * SUBS, attend, 0)
    o_t = (acc_o[...] * inv).astype(BF16)
    delta = jnp.sum(o_t.astype(F32) * dot_t[...].astype(F32), axis=0, keepdims=True) * inv
    for h in range(G):
        cols = slice(h * HW, (h + 1) * HW)
        o_rows[:, cols] = o_t[:, cols].astype(F32).T.astype(BF16)

    def key_grad(c, p):
        gp = dot(part_of(vb, c, p), dot_t[...])
        gs = (eb[c, p].astype(F32) * (gp * inv - delta)).astype(BF16)
        acc_q[...] += lax.dot_general(part_of(kb, c, p), gs, TN, preferred_element_type=F32)
        g = dot(gs, qn[...]) * scale
        pk[c, pl.ds(2 * p, 2)] = g.astype(BF16).reshape(2, HW, HW)
        for j in range(4):
            t = g[j * BLK:(j + 1) * BLK]
            back = t * cos_i - turn(t) * sin_i
            row = block_row(c, 2 * p + j // 2) * 2 + j % 2
            ub[pl.ds(row, 1), :] = jnp.sum(back, axis=0, keepdims=True)

    over(chunks_at(HY), key_grad)
    k_r = scatter_step(*k_bufs, 0)

    def mix(n, carry):
        half = n // n_inner
        at = pl.multiple_of(lax.rem(n, n_inner) * CHUNK, CHUNK)
        r = dot(o_rows[...], wb[half, :, pl.ds(at, CHUNK)]).astype(BF16)
        to = pl.multiple_of(n * CHUNK, CHUNK)
        po[:, :, :, pl.ds(to, CHUNK)] = r.reshape(NZL, NX, HW // (NZL * NX), CHUNK)
        return carry

    x_far, x_up, x_down = (lax.rem(x + d, NX) for d in (HX, 1, NX - 1))

    for k in range(1, HY):
        if k < HY - 1:
            over(chunks_at(HY - 1 - k), value_grad)
            take(*v_bufs, k, v_r)
            v_r = scatter_step(*v_bufs, k + 1)
        if k == 1:
            lax.fori_loop(0, 2 * n_inner, mix, 0)
            o_far = [
                wires.start(po.at[:, x_far, :, left], rx_half.at[0], x_peer(1)),
                wires.start(po.at[:, x_far, :, right], rx_half.at[1], x_peer(-1)),
            ]
        over(chunks_at(HY - k), key_grad)
        take(*k_bufs, k - 1, k_r)
        k_r = scatter_step(*k_bufs, k)
        if k == 2 or HY == 2:
            arrived(o_far)
            po[:, x_up, :, left] = (po[:, x_up, :, left].astype(F32) + rx_half[0].astype(F32)).astype(BF16)
            po[:, x_down, :, right] = (po[:, x_down, :, right].astype(F32) + rx_half[1].astype(F32)).astype(BF16)
            o_near = [
                wires.start(po.at[:, x_up], rx_full.at[0], x_peer(1)),
                wires.start(po.at[:, x_down], rx_full.at[1], x_peer(-1)),
            ]
    over(chunks_at(0), value_grad)
    over(chunks_at(0), key_grad)

    take(*v_bufs, HY - 1, v_r)
    v_zr = [wires.start(pv.at[0, r], rv_z.at[r - 1], z_peer(r)) for r in range(1, NZ)]

    for h in range(G):
        cols = slice(h * HW, (h + 1) * HW)
        g = acc_q[:, cols].T * scale
        g = g * cos - turn(g) * sin
        qg_ref[0, :, cols] = g.astype(BF16)
        btile[0, h:h + 1, :] = jnp.sum(g, axis=0, keepdims=True)
    base_angle = bpv[...].astype(F32) * freq
    u = ub[...]
    u = u * jnp.cos(base_angle) - turn(u) * (jnp.sin(base_angle) * sign)
    btile[0, G:G + 1, :] = jnp.sum(u, axis=0, keepdims=True)
    btile[0, G + 1:G + 2, :] = jnp.sum(vs[...], axis=0, keepdims=True)
    btile[0, G + 2:8, :] = jnp.zeros((8 - G - 2, HW), F32)
    bias_dp = wires.start(btile.at[0], b_dp, dp_peer)

    take(*k_bufs, HY - 1, k_r)
    k_zr = [wires.start(pk.at[0, r], rk_z.at[r - 1], z_peer(r)) for r in range(1, NZ)]

    bias_dp.wait_recv()
    btile[1] = btile[0] + b_dp[...]
    bias_z = [wires.start(btile.at[1], b_z.at[r - 1], z_peer(r)) for r in range(1, NZ)]

    arrived(o_near)
    other = 1 - zl
    zs[...] = (
        po[other, x].astype(F32) + rx_full[0, other].astype(F32) + rx_full[1, other].astype(F32)
    ).astype(BF16)
    o_z = wires.start(zs, rz, zl_peer)

    arrived(bias_z)
    total = btile[1]
    for r in range(NZ - 1):
        total = total + b_z[r]
    btile[2] = total
    bias_y = [wires.start(btile.at[2], b_y.at[d - 1], y_peer(d)) for d in range(1, NY)]

    arrived(v_zr)
    g = pv[0, 0].astype(F32)
    for r in range(NZ - 1):
        g = g + rv_z[r].astype(F32)
    vg_ref[0] = g.astype(BF16)

    o_z.wait_recv()
    out_ref[0] = (
        po[zl, x].astype(F32)
        + rx_full[0, zl].astype(F32)
        + rx_full[1, zl].astype(F32)
        + rz[...].astype(F32)
    ).astype(BF16)

    arrived(k_zr)
    g = pk[0, 0].astype(F32)
    for r in range(NZ - 1):
        g = g + rk_z[r].astype(F32)
    kg_ref[0] = (g * cos - turn(g) * sin).astype(BF16)

    arrived(bias_y)
    for d in range(NY - 1):
        total = total + b_y[d]
    bias_ref[...] = total
    wires.finish()


def layer(mesh_shape, q_in, key_input, value_input, q_bias, key_bias, value_bias, out_weight, out_grad, doc_lengths, block_pos):
    NY, NX = mesh_shape["ctx"] // NZ, mesh_shape["tp"] // NZL
    rows, features = q_in.shape[1:]
    G = features // HW
    own_rows, width = out_grad.shape[1:]
    w_cols = out_weight.shape[1]
    QN = G * HW
    SUBS, ROWS = NZ // 2, 4 * BLK
    freq = ROPE_BASE ** (-np.arange(0, HW, 2, dtype=np.float64) / HW)
    freq = jnp.asarray(np.concatenate([freq, freq])[None].astype(np.float32))
    vmem, anywhere = pl.BlockSpec(memory_space=pltpu.VMEM), pl.BlockSpec(memory_space=pl.ANY)
    smem = pl.BlockSpec(memory_space=pltpu.SMEM)
    V = pltpu.VMEM
    HY = NY // 2
    ring = [V((2, NZ // 2, HW, HW), BF16), V((HY - 1, 2, NZ, HW, HW), BF16), V((NZ - 1, HW, HW), BF16)]
    copies = 2 * (NZ - 1 + 2 * HY) + 1 + 9 + 2 * (2 * HY + NZ - 1) + 5 + 1 + NZ - 1 + NY - 1
    outs = pl.pallas_call(
        functools.partial(kernel, (NY, NX, G)),
        out_shape=(
            jax.ShapeDtypeStruct((1, own_rows, width), BF16),
            jax.ShapeDtypeStruct((1, rows, features), BF16),
            jax.ShapeDtypeStruct((1, rows, HW), BF16),
            jax.ShapeDtypeStruct((1, rows, HW), BF16),
            jax.ShapeDtypeStruct((8, HW), F32),
        ),
        in_specs=[vmem] * 7 + [smem] * 2 + [anywhere] * 2,
        out_specs=(vmem,) * 5,
        scratch_shapes=[
            V((QN, HW), BF16),
            V((HW, QN), BF16),
            V((NY, NZ, HW, HW), BF16),
            V((NY, NZ, HW, HW), BF16),
            V((NY, SUBS, ROWS, QN), F32),
            V((NY, SUBS, ROWS, QN), BF16),
            V((2, features, w_cols), BF16),
            V((NZL * NX, own_rows, width), BF16),
            V((HW, QN), BF16),
            V((QN, HW), BF16),
            V((HW, QN), BF16),
            V((HW, QN), F32),
            V((HW, QN), F32),
            V((QN, HW), F32),
            V((NY, NZ, HW, HW), BF16),
            V((NY, NZ, HW, HW), BF16),
            *ring,
            *ring,
            V((NZL, NX, own_rows, width), BF16),
            V((2, NZL, own_rows, w_cols), BF16),
            V((2, NZL, own_rows, width), BF16),
            V((own_rows, width), BF16),
            V((own_rows, width), BF16),
            V((8, QN), F32),
            V((8, QN), F32),
            V((2 * NZ * NY, HW), F32),
            V((2 * NZ * NY, HW), jnp.int32),
            V((8, HW), F32),
            V((3, 8, HW), F32),
            V((8, HW), F32),
            V((NZ - 1, 8, HW), F32),
            V((NY - 1, 8, HW), F32),
            pltpu.SemaphoreType.DMA((2,)),
            pltpu.SemaphoreType.DMA((copies,)),
            pltpu.SemaphoreType.DMA((copies,)),
        ],
        compiler_params=pltpu.CompilerParams(
            collective_id=0, has_side_effects=True, vmem_limit_bytes=60 * 1024 * 1024
        ),
        name="attention_layer",
    )(
        q_in, key_input, value_input, q_bias.reshape(1, -1), key_bias.reshape(1, -1),
        value_bias.reshape(1, -1), freq, block_pos, doc_lengths, out_weight, out_grad[0],
    )
    out, q_grad, k_grad, v_grad, bias = outs
    return (out, q_grad, k_grad, v_grad, bias[:G].reshape(-1), bias[G], bias[G + 1])


def solution(mesh):
    return jax.shard_map(
        functools.partial(layer, dict(mesh.shape)),
        mesh=mesh,
        in_specs=(
            P("dp", "ctx", "tp"),
            P("dp", "ctx", "tp"),
            P("dp", "ctx", "tp"),
            P("tp"),
            P("tp"),
            P("tp"),
            P("tp", "dp"),
            P("dp", ("ctx", "tp"), None),
            P("dp", None),
            P("dp", None, None),
        ),
        out_specs=(
            P("dp", ("ctx", "tp"), None),
            P("dp", "ctx", "tp"),
            P("dp", "ctx", "tp"),
            P("dp", "ctx", "tp"),
            P("tp"),
            P("tp"),
            P("tp"),
        ),
        check_vma=False,
    )
```

```python
import functools

import jax
import jax.numpy as jnp
import numpy as np
from jax import lax
from jax.experimental import pallas as pl
from jax.experimental.pallas import tpu as pltpu
from jax.sharding import PartitionSpec as P

HW = 128
HALF = HW // 2
BLK = 64
ROPE_BASE = 1000000.0
NZ = 4
NZL = 2
CHUNK = 512
LOW = -1e30
LOG2E = 1.4426950408889634
MESH = pl.DeviceIdType.MESH
F32 = jnp.float32
BF16 = jnp.bfloat16
NT = (((1,), (1,)), ((), ()))
TN = (((0,), (0,)), ((), ()))


def dot(a, b):
    return jnp.dot(a, b, preferred_element_type=F32)


def turn(x):
    return pltpu.roll(x, HALF, 1)


class Wires:
    def __init__(self, send, recv):
        self.send, self.recv, self.all = send, recv, []

    def start(self, src, dst, target):
        n = len(self.all)
        copy = pltpu.make_async_remote_copy(
            src_ref=src,
            dst_ref=dst,
            send_sem=self.send.at[n],
            recv_sem=self.recv.at[n],
            device_id=target,
            device_id_type=MESH,
        )
        copy.start()
        self.all.append(copy)
        return copy

    def finish(self):
        for copy in self.all:
            copy.wait_send()


class Term:
    def __init__(self, buf, slots, landing):
        self.buf, self.slots, self.landing = buf, slots, landing
        self.out, self.last = {}, []


def kernel(
    dims,
    q_ref, k_ref, v_ref, qb_ref, kbias_ref, vbias_ref, freq_ref, bp_ref, doc_ref, w_hbm, og_hbm,
    out_ref, qg_ref, kg_ref, vg_ref, bias_ref,
    qn, qt, kb, vb, sb, eb, wb, og, dot_t, dot_n, o_rows, acc_o, acc_q, acc_g,
    pk, pv, rk, rk_z, rv, rv_z,
    po, rx_half, rx_full, rz, zs, mb, lb, ub, bpv, vs, btile, b_dp, b_z, b_y,
    local_sem, send_sem, recv_sem,
):
    NY, NX, G = dims
    ctx, tp, dp = lax.axis_index("ctx"), lax.axis_index("tp"), lax.axis_index("dp")
    z, y = ctx // NY, lax.rem(ctx, NY)
    zl, x = tp // NX, lax.rem(tp, NX)
    HY, HX = NY // 2, NX // 2
    QN = G * HW
    ROWS = NZ * HW

    def y_peer(d):
        return {"ctx": z * NY + lax.rem(y + d + NY, NY)}

    def z_peer(d):
        return {"ctx": lax.rem(z + d, NZ) * NY + y}

    def x_peer(d):
        return {"tp": zl * NX + lax.rem(x + d + NX, NX)}

    zl_peer = {"tp": (1 - zl) * NX + x}
    dp_peer = {"dp": 1 - dp}

    barrier = pltpu.get_barrier_semaphore()
    peers = [y_peer(d) for d in range(1, NY)] + [z_peer(d) for d in range(1, NZ)]
    peers += [x_peer(1), x_peer(-1), zl_peer, dp_peer]
    for peer in peers:
        pl.semaphore_signal(barrier, inc=1, device_id=peer, device_id_type=MESH)

    own_w = pltpu.make_async_copy(w_hbm, wb.at[dp], local_sem.at[0])
    own_w.start()
    own_g = pltpu.make_async_copy(og_hbm, og.at[tp], local_sem.at[1])
    own_g.start()

    b0, b1 = bp_ref[0, 0, ctx] * BLK, bp_ref[0, 1, ctx] * BLK
    sub = lax.broadcasted_iota(jnp.int32, (HW, HW), 0)
    pos = jnp.where(sub < BLK, b0 + sub, b1 + (sub - BLK))
    freq = freq_ref[...]
    angle = pos.astype(F32) * freq
    sign = jnp.where(lax.broadcasted_iota(jnp.int32, (1, HW), 1) < HALF, -1.0, 1.0)
    cos, sin = jnp.cos(angle), jnp.sin(angle) * sign
    inner = lax.broadcasted_iota(jnp.int32, (BLK, HW), 0).astype(F32) * freq
    cos_i, sin_i = jnp.cos(inner), jnp.sin(inner) * sign

    xk = k_ref[0].astype(F32) + kbias_ref[...]
    kb[0, 0] = (xk * cos + turn(xk) * sin).astype(BF16)
    vb[0, 0] = (v_ref[0].astype(F32) + vbias_ref[...]).astype(BF16)

    pl.semaphore_wait(barrier, len(peers))
    wires = Wires(send_sem, recv_sem)

    lower = range(NZ // 2)
    order = [1, 3, 2][:NZ - 1] if NZ > 2 else [1]

    def arrived(copies):
        for copy in copies:
            copy.wait_recv()

    def hop(buf, k, r):
        last = k == HY
        copies = []
        if not last or r in lower:
            copies.append(wires.start(buf.at[(NY - k + 1) % NY, r], buf.at[NY - k, r], y_peer(1)))
        if not last or r not in lower:
            copies.append(wires.start(buf.at[k - 1, r], buf.at[k, r], y_peer(-1)))
        return copies

    def forward(buf, seen, k, chains):
        for r in chains:
            arrived(seen[k, r])
            seen[k + 1, r] = hop(buf, k + 1, r)

    k_in, v_in = {}, {}
    for r in order:
        k_in[0, r] = [wires.start(kb.at[0, 0], kb.at[0, r], z_peer(NZ - r))]
    k_in[1, 0] = hop(kb, 1, 0)
    g_x = [wires.start(og_hbm, og.at[tp], x_peer(d)) for d in (1, -1)]
    g_z = wires.start(og_hbm, og.at[tp], zl_peer)
    for r in order:
        v_in[0, r] = [wires.start(vb.at[0, 0], vb.at[0, r], z_peer(NZ - r))]
    v_in[1, 0] = hop(vb, 1, 0)
    far_w = wires.start(w_hbm, wb.at[dp], dp_peer)

    for h in range(G):
        cols = slice(h * HW, (h + 1) * HW)
        xq = q_ref[0, :, cols].astype(F32) + qb_ref[cols][None, :]
        rq = xq * cos + turn(xq) * sin
        qn[cols, :] = rq.astype(BF16)
        qt[:, cols] = rq.T.astype(BF16)
    lane = lax.broadcasted_iota(jnp.int32, (1, HW), 1)
    row_pos = jnp.where(lane < BLK, b0 + lane, b1 + (lane - BLK))
    end = jnp.int32(0)
    row_start = jnp.zeros((1, HW), jnp.int32)
    for d in range(doc_ref.shape[1]):
        row_start = jnp.where(row_pos >= end, end, row_start)
        end = end + doc_ref[0, d]
    row_pos = jnp.concatenate([row_pos] * G, axis=1)
    row_start = jnp.concatenate([row_start] * G, axis=1)
    mb[...] = jnp.full(mb.shape, LOW, F32)
    lb[...] = jnp.zeros(lb.shape, F32)
    vs[...] = jnp.zeros(vs.shape, F32)
    acc_o[...] = jnp.zeros(acc_o.shape, F32)
    acc_q[...] = jnp.zeros(acc_q.shape, F32)
    acc_g[...] = jnp.zeros(acc_g.shape, F32)

    def block_row(c, r):
        return lax.rem(z + r, NZ) * NY + lax.rem(y + c, NY)

    def base_step(i, carry):
        for h in range(2):
            bpv[pl.ds(2 * i + h, 1), :] = jnp.full((1, HW), bp_ref[0, h, i] * BLK, jnp.int32)
        return carry

    lax.fori_loop(0, NZ * NY, base_step, 0)

    def over(chunks, body):
        def step(i, carry):
            body(chunks[0] + i * (chunks[-1] - chunks[0]))
            return carry

        lax.fori_loop(0, len(chunks), step, 0)

    def whole(ref, c):
        return ref[c].reshape(ROWS, HW)

    def score(c):
        s = dot(whole(kb, c), qt[...])
        spot = lax.broadcasted_iota(jnp.int32, (BLK, QN), 0)
        most = mb[...]
        for j in range(2 * NZ):
            base = bp_ref[0, j % 2, block_row(c, j // 2)] * BLK
            piece = s[j * BLK:(j + 1) * BLK]
            piece = jnp.where((spot <= row_pos - base) & (spot >= row_start - base), piece, LOW)
            sb[c, j * BLK:(j + 1) * BLK, :] = piece
            most = jnp.maximum(most, jnp.max(piece.reshape(BLK // 8, 8, QN), axis=0))
        mb[...] = most

    def chunks_at(k):
        return [0] if k == 0 else [HY] if k == HY else [k, NY - k]

    w_cols = wb.shape[2]
    left, right = pl.ds(0, w_cols), pl.ds(w_cols, w_cols)

    def opposite(line):
        from_left = zl_line(line) + lax.rem(x + NX - 1, NX)
        from_right = zl_line(line) + lax.rem(x + 1, NX)
        return [
            wires.start(og.at[from_left, :, left], og.at[from_left, :, left], x_peer(1)),
            wires.start(og.at[from_right, :, right], og.at[from_right, :, right], x_peer(-1)),
        ]

    def zl_line(line):
        return (zl if line == 0 else 1 - zl) * NX

    own = [0]
    forward(kb, k_in, 1, own)
    forward(vb, v_in, 1, own)
    forward(kb, k_in, 0, order)
    arrived(g_x)
    g_half = opposite(0)
    if HY > 2:
        forward(kb, k_in, 2, own)
        forward(vb, v_in, 2, own)
    over(chunks_at(0), score)
    g_z.wait_recv()
    partner = zl_line(1) + x
    g_next = [wires.start(og.at[partner], og.at[partner], x_peer(d)) for d in (1, -1)]
    if HY > 3:
        forward(kb, k_in, 3, own)
        forward(vb, v_in, 3, own)
    for k in range(1, HY):
        forward(kb, k_in, k, order)
        over(chunks_at(k), score)
        forward(vb, v_in, k - 1, order)
        if k == 2 or HY == 2:
            arrived(g_next)
            g_last = opposite(1)

    own_g.wait()
    own_w.wait()
    n_inner = w_cols // CHUNK

    def project(half):
        def step(n, carry):
            w = wb[half, :, pl.ds(pl.multiple_of(n * CHUNK, CHUNK), CHUNK)]
            at = pl.multiple_of(half * w_cols + n * CHUNK, CHUNK)
            g = og[:, :, pl.ds(at, CHUNK)].reshape(HW, CHUNK)
            acc_g[...] += lax.dot_general(w, g, NT, preferred_element_type=F32)
            return carry

        lax.fori_loop(0, n_inner, step, 0)

    arrived(g_half)
    arrived(g_last)
    project(dp)
    far_w.wait_recv()
    project(1 - dp)
    for h in range(G):
        dot_t[:, h * HW:(h + 1) * HW] = acc_g[h * HW:(h + 1) * HW, :].astype(BF16)

    for r in range(NZ):
        arrived(k_in[HY, r])
    over(chunks_at(HY), score)
    forward(vb, v_in, HY - 1, order)

    scale = HW ** -0.5
    top = jnp.max(mb[...], axis=0, keepdims=True) * (scale * LOG2E)

    def soften(c, carry):
        total = lb[...]
        for j in range(2 * NZ):
            rows = slice(j * BLK, (j + 1) * BLK)
            e = jnp.exp2(sb[c, rows, :] * (scale * LOG2E) - top)
            total = total + jnp.sum(e.reshape(BLK // 8, 8, QN), axis=0)
            eb[c, rows, :] = e.astype(BF16)
        lb[...] = total
        return carry

    lax.fori_loop(0, NY, soften, 0)
    inv = 1.0 / jnp.sum(lb[...], axis=0, keepdims=True)
    for h in range(G):
        cols = slice(h * HW, (h + 1) * HW)
        scaled = dot_t[:, cols].astype(F32) * inv[:, cols]
        dot_n[cols, :] = scaled.T.astype(BF16)

    def value_grad(c):
        g = dot(eb[c], dot_n[...])
        vs[...] += jnp.sum(g.reshape(ROWS // 8, 8, HW), axis=0)
        pv[c] = g.astype(BF16).reshape(NZ, HW, HW)

    def attend(c):
        acc_o[...] += lax.dot_general(whole(vb, c), eb[c], TN, preferred_element_type=F32)

    def send_terms(term, r, up, down, k):
        if up:
            term.out[k, r, 0] = wires.start(term.buf.at[HY - k, r], term.slots.at[k, 0, r], y_peer(1))
        if down:
            term.out[k, r, 1] = wires.start(term.buf.at[HY + k, r], term.slots.at[k, 1, r], y_peer(-1))

    def scatter(term, k):
        for r in range(NZ):
            for way, c in ((0, HY - k), (1, HY + k)):
                if (k - 1, r, way) in term.out:
                    term.out[k - 1, r, way].wait_recv()
                    term.buf[c, r] = (term.buf[c, r].astype(F32) + term.slots[k - 1, way, r].astype(F32)).astype(BF16)
            send_terms(term, r, k > 0 or r in lower, k > 0 or r not in lower, k)

    def settle(term):
        for r in order + [0]:
            arrived([term.out[HY - 1, r, way] for way in (0, 1)])
            both = term.slots[HY - 1, 0, r].astype(F32) + term.slots[HY - 1, 1, r].astype(F32)
            term.buf[0, r] = (term.buf[0, r].astype(F32) + both).astype(BF16)
            if r:
                term.last.append(wires.start(term.buf.at[0, r], term.landing.at[r - 1], z_peer(r)))

    def total_of(term):
        arrived(term.last)
        g = term.buf[0, 0].astype(F32)
        for r in range(NZ - 1):
            g = g + term.landing[r].astype(F32)
        return g

    v_term, k_term = Term(pv, rv, rv_z), Term(pk, rk, rk_z)

    over(chunks_at(HY), value_grad)
    scatter(v_term, 0)
    over(chunks_at(HY - 1), value_grad)
    scatter(v_term, 1)
    if HY > 2:
        over(chunks_at(HY - 2), value_grad)
    for k in range(HY):
        over(chunks_at(k), attend)
    if HY > 2:
        scatter(v_term, 2)
    for k in range(1, HY - 2):
        over(chunks_at(k), value_grad)
    for r in range(NZ):
        arrived(v_in[HY, r])
    over(chunks_at(HY), attend)
    o_t = (acc_o[...] * inv).astype(BF16)
    delta = jnp.sum(o_t.astype(F32) * dot_t[...].astype(F32), axis=0, keepdims=True) * inv
    for h in range(G):
        cols = slice(h * HW, (h + 1) * HW)
        o_rows[:, cols] = o_t[:, cols].astype(F32).T.astype(BF16)

    def key_grad(c):
        gp = dot(whole(vb, c), dot_t[...])
        gs = (eb[c].astype(F32) * (gp * inv - delta)).astype(BF16)
        acc_q[...] += lax.dot_general(whole(kb, c), gs, TN, preferred_element_type=F32)
        g = dot(gs, qn[...]) * scale
        pk[c] = g.astype(BF16).reshape(NZ, HW, HW)
        for j in range(2 * NZ):
            t = g[j * BLK:(j + 1) * BLK]
            back = t * cos_i - turn(t) * sin_i
            row = block_row(c, j // 2) * 2 + j % 2
            ub[pl.ds(row, 1), :] = jnp.sum(back, axis=0, keepdims=True)

    over(chunks_at(HY), key_grad)
    scatter(k_term, 0)
    for k in range(3, HY):
        scatter(v_term, k)

    def mix(n, carry):
        half = n // n_inner
        at = pl.multiple_of(lax.rem(n, n_inner) * CHUNK, CHUNK)
        r = dot(o_rows[...], wb[half, :, pl.ds(at, CHUNK)]).astype(BF16)
        to = pl.multiple_of(n * CHUNK, CHUNK)
        po[:, :, :, pl.ds(to, CHUNK)] = r.reshape(NZL, NX, HW // (NZL * NX), CHUNK)
        return carry

    x_far, x_up, x_down = (lax.rem(x + d, NX) for d in (HX, 1, NX - 1))

    lax.fori_loop(0, 2 * n_inner, mix, 0)
    o_far = [
        wires.start(po.at[:, x_far, :, left], rx_half.at[0], x_peer(1)),
        wires.start(po.at[:, x_far, :, right], rx_half.at[1], x_peer(-1)),
    ]
    for k in range(1, HY):
        over(chunks_at(HY - k), key_grad)
        scatter(k_term, k)
        if k == 1:
            over(chunks_at(0), value_grad)
            settle(v_term)
        if k == 2 or HY == 2:
            arrived(o_far)
            po[:, x_up, :, left] = (po[:, x_up, :, left].astype(F32) + rx_half[0].astype(F32)).astype(BF16)
            po[:, x_down, :, right] = (po[:, x_down, :, right].astype(F32) + rx_half[1].astype(F32)).astype(BF16)
            o_near = [
                wires.start(po.at[:, x_up], rx_full.at[0], x_peer(1)),
                wires.start(po.at[:, x_down], rx_full.at[1], x_peer(-1)),
            ]
    over(chunks_at(0), key_grad)

    for h in range(G):
        cols = slice(h * HW, (h + 1) * HW)
        g = acc_q[:, cols].T * scale
        g = g * cos - turn(g) * sin
        qg_ref[0, :, cols] = g.astype(BF16)
        btile[0, h:h + 1, :] = jnp.sum(g, axis=0, keepdims=True)
    base_angle = bpv[...].astype(F32) * freq
    u = ub[...]
    u = u * jnp.cos(base_angle) - turn(u) * (jnp.sin(base_angle) * sign)
    btile[0, G:G + 1, :] = jnp.sum(u, axis=0, keepdims=True)
    btile[0, G + 1:G + 2, :] = jnp.sum(vs[...], axis=0, keepdims=True)
    btile[0, G + 2:8, :] = jnp.zeros((8 - G - 2, HW), F32)
    bias_dp = wires.start(btile.at[0], b_dp, dp_peer)

    settle(k_term)

    bias_dp.wait_recv()
    btile[1] = btile[0] + b_dp[...]
    bias_z = [wires.start(btile.at[1], b_z.at[r - 1], z_peer(r)) for r in range(1, NZ)]

    arrived(o_near)
    other = 1 - zl
    zs[...] = (
        po[other, x].astype(F32) + rx_full[0, other].astype(F32) + rx_full[1, other].astype(F32)
    ).astype(BF16)
    o_z = wires.start(zs, rz, zl_peer)

    arrived(bias_z)
    total = btile[1]
    for r in range(NZ - 1):
        total = total + b_z[r]
    btile[2] = total
    bias_y = [wires.start(btile.at[2], b_y.at[d - 1], y_peer(d)) for d in range(1, NY)]

    vg_ref[0] = total_of(v_term).astype(BF16)

    o_z.wait_recv()
    out_ref[0] = (
        po[zl, x].astype(F32)
        + rx_full[0, zl].astype(F32)
        + rx_full[1, zl].astype(F32)
        + rz[...].astype(F32)
    ).astype(BF16)

    g = total_of(k_term)
    kg_ref[0] = (g * cos - turn(g) * sin).astype(BF16)

    arrived(bias_y)
    for d in range(NY - 1):
        total = total + b_y[d]
    bias_ref[...] = total
    wires.finish()


def layer(mesh_shape, q_in, key_input, value_input, q_bias, key_bias, value_bias, out_weight, out_grad, doc_lengths, block_pos):
    NY, NX = mesh_shape["ctx"] // NZ, mesh_shape["tp"] // NZL
    rows, features = q_in.shape[1:]
    G = features // HW
    own_rows, width = out_grad.shape[1:]
    w_cols = out_weight.shape[1]
    QN = G * HW
    ROWS = NZ * HW
    freq = ROPE_BASE ** (-np.arange(0, HW, 2, dtype=np.float64) / HW)
    freq = jnp.asarray(np.concatenate([freq, freq])[None].astype(np.float32))
    vmem, anywhere = pl.BlockSpec(memory_space=pltpu.VMEM), pl.BlockSpec(memory_space=pl.ANY)
    smem = pl.BlockSpec(memory_space=pltpu.SMEM)
    V = pltpu.VMEM
    HY = NY // 2
    ring = [V((HY, 2, NZ, HW, HW), BF16), V((NZ - 1, HW, HW), BF16)]
    copies = 4 * (NZ - 1 + NZ * (2 * HY - 1)) + 16 + NZ + NY
    outs = pl.pallas_call(
        functools.partial(kernel, (NY, NX, G)),
        out_shape=(
            jax.ShapeDtypeStruct((1, own_rows, width), BF16),
            jax.ShapeDtypeStruct((1, rows, features), BF16),
            jax.ShapeDtypeStruct((1, rows, HW), BF16),
            jax.ShapeDtypeStruct((1, rows, HW), BF16),
            jax.ShapeDtypeStruct((8, HW), F32),
        ),
        in_specs=[vmem] * 7 + [smem] * 2 + [anywhere] * 2,
        out_specs=(vmem,) * 5,
        scratch_shapes=[
            V((QN, HW), BF16),
            V((HW, QN), BF16),
            V((NY, NZ, HW, HW), BF16),
            V((NY, NZ, HW, HW), BF16),
            V((NY, ROWS, QN), F32),
            V((NY, ROWS, QN), BF16),
            V((2, features, w_cols), BF16),
            V((NZL * NX, own_rows, width), BF16),
            V((HW, QN), BF16),
            V((QN, HW), BF16),
            V((HW, QN), BF16),
            V((HW, QN), F32),
            V((HW, QN), F32),
            V((QN, HW), F32),
            V((NY, NZ, HW, HW), BF16),
            V((NY, NZ, HW, HW), BF16),
            *ring,
            *ring,
            V((NZL, NX, own_rows, width), BF16),
            V((2, NZL, own_rows, w_cols), BF16),
            V((2, NZL, own_rows, width), BF16),
            V((own_rows, width), BF16),
            V((own_rows, width), BF16),
            V((8, QN), F32),
            V((8, QN), F32),
            V((2 * NZ * NY, HW), F32),
            V((2 * NZ * NY, HW), jnp.int32),
            V((8, HW), F32),
            V((3, 8, HW), F32),
            V((8, HW), F32),
            V((NZ - 1, 8, HW), F32),
            V((NY - 1, 8, HW), F32),
            pltpu.SemaphoreType.DMA((2,)),
            pltpu.SemaphoreType.DMA((copies,)),
            pltpu.SemaphoreType.DMA((copies,)),
        ],
        compiler_params=pltpu.CompilerParams(
            collective_id=0, has_side_effects=True, vmem_limit_bytes=60 * 1024 * 1024
        ),
        name="attention_layer",
    )(
        q_in, key_input, value_input, q_bias, key_bias.reshape(1, -1),
        value_bias.reshape(1, -1), freq, jnp.swapaxes(block_pos, 1, 2), doc_lengths, out_weight, out_grad[0],
    )
    shapes = [jax.ShapeDtypeStruct(o.shape, o.dtype) for o in outs[:4]]
    shapes += [jax.ShapeDtypeStruct((n,), F32) for n in (features, HW, HW)]
    return pl.pallas_call(
        functools.partial(finish, G),
        out_shape=tuple(shapes),
        in_specs=[vmem] * 5,
        out_specs=(vmem,) * 7,
        compiler_params=pltpu.CompilerParams(vmem_limit_bytes=60 * 1024 * 1024),
        name="hand_over",
    )(*outs)


def finish(G, *refs):
    bias_ref, biases = refs[4], refs[9:]
    for source, target in zip(refs[:4], refs[5:9]):
        target[...] = source[...]
    for h in range(G):
        biases[0][h * HW:(h + 1) * HW] = bias_ref[h]
    biases[1][...] = bias_ref[G]
    biases[2][...] = bias_ref[G + 1]


def solution(mesh):
    return jax.shard_map(
        functools.partial(layer, dict(mesh.shape)),
        mesh=mesh,
        in_specs=(
            P("dp", "ctx", "tp"),
            P("dp", "ctx", "tp"),
            P("dp", "ctx", "tp"),
            P("tp"),
            P("tp"),
            P("tp"),
            P("tp", "dp"),
            P("dp", ("ctx", "tp"), None),
            P("dp", None),
            P("dp", None, None),
        ),
        out_specs=(
            P("dp", ("ctx", "tp"), None),
            P("dp", "ctx", "tp"),
            P("dp", "ctx", "tp"),
            P("dp", "ctx", "tp"),
            P("tp"),
            P("tp"),
            P("tp"),
        ),
        check_vma=False,
    )
```

```python
import functools

import jax
import jax.numpy as jnp
import numpy as np
from jax import lax
from jax.experimental import pallas as pl
from jax.experimental.pallas import tpu as pltpu
from jax.sharding import PartitionSpec as P

HW = 128
HALF = HW // 2
BLK = 64
ROPE_BASE = 1000000.0
NZ = 4
NZL = 2
CHUNK = 512
LOW = -1e30
LOG2E = 1.4426950408889634
MESH = pl.DeviceIdType.MESH
F32 = jnp.float32
BF16 = jnp.bfloat16
NT = (((1,), (1,)), ((), ()))
TN = (((0,), (0,)), ((), ()))


def dot(a, b):
    return jnp.dot(a, b, preferred_element_type=F32)


def turn(x):
    return pltpu.roll(x, HALF, 1)


class Wires:
    def __init__(self, send, recv):
        self.send, self.recv, self.all = send, recv, []

    def start(self, src, dst, target):
        n = len(self.all)
        copy = pltpu.make_async_remote_copy(
            src_ref=src,
            dst_ref=dst,
            send_sem=self.send.at[n],
            recv_sem=self.recv.at[n],
            device_id=target,
            device_id_type=MESH,
        )
        copy.start()
        self.all.append(copy)
        return copy

    def finish(self):
        for copy in self.all:
            copy.wait_send()


def near_and_far(n):
    away = [[n // 2]] + [[d, n - d] for d in range(n // 2 - 1, 0, -1)]
    near = [c for pair in away for c in pair if pair[0] <= n // 4]
    return near, [c for pair in away for c in pair if pair[0] > n // 4]


def pairs(chunks):
    odd = len(chunks) % 2
    return [chunks[:1]] * odd + [chunks[i:i + 2] for i in range(odd, len(chunks), 2)]


class Direct:
    def __init__(self, buf, slots, far_slots, middle, landing):
        self.buf, self.slots, self.far_slots = buf, slots, far_slots
        self.middle, self.landing = middle, landing
        self.first, self.direct, self.last = {}, [], []


class Term:
    def __init__(self, buf, slots, landing):
        self.buf, self.slots, self.landing = buf, slots, landing
        self.out, self.last = {}, []


def kernel(
    dims,
    q_ref, k_ref, v_ref, qb_ref, kbias_ref, vbias_ref, freq_ref, bp_ref, doc_ref, w_hbm, og_hbm,
    out_ref, qg_ref, kg_ref, vg_ref, bias_ref,
    qn, qt, kb, vb, sb, eb, wb, og, dot_t, dot_n, o_rows, acc_o, acc_q, acc_g,
    pk, pv, rk, rk_f, rk_m, rk_z, rv, rv_z,
    po, rx_half, rx_full, rz, zs, mb, lb, ub, bpv, vs, btile, b_dp, b_z, b_y,
    local_sem, send_sem, recv_sem,
):
    NY, NX, G = dims
    ctx, tp, dp = lax.axis_index("ctx"), lax.axis_index("tp"), lax.axis_index("dp")
    z, y = ctx // NY, lax.rem(ctx, NY)
    zl, x = tp // NX, lax.rem(tp, NX)
    HY, HX = NY // 2, NX // 2
    QN = G * HW
    ROWS = NZ * HW

    def y_peer(d):
        return {"ctx": z * NY + lax.rem(y + d + NY, NY)}

    def z_peer(d):
        return {"ctx": lax.rem(z + d, NZ) * NY + y}

    def x_peer(d):
        return {"tp": zl * NX + lax.rem(x + d + NX, NX)}

    zl_peer = {"tp": (1 - zl) * NX + x}
    dp_peer = {"dp": 1 - dp}

    barrier = pltpu.get_barrier_semaphore()
    peers = [y_peer(d) for d in range(1, NY)] + [z_peer(d) for d in range(1, NZ)]
    peers += [x_peer(1), x_peer(-1), zl_peer, dp_peer]
    for peer in peers:
        pl.semaphore_signal(barrier, inc=1, device_id=peer, device_id_type=MESH)

    own_w = pltpu.make_async_copy(w_hbm, wb.at[dp], local_sem.at[0])
    own_w.start()
    own_g = pltpu.make_async_copy(og_hbm, og.at[tp], local_sem.at[1])
    own_g.start()

    b0, b1 = bp_ref[0, 0, ctx] * BLK, bp_ref[0, 1, ctx] * BLK
    sub = lax.broadcasted_iota(jnp.int32, (HW, HW), 0)
    pos = jnp.where(sub < BLK, b0 + sub, b1 + (sub - BLK))
    freq = freq_ref[...]
    angle = pos.astype(F32) * freq
    sign = jnp.where(lax.broadcasted_iota(jnp.int32, (1, HW), 1) < HALF, -1.0, 1.0)
    cos, sin = jnp.cos(angle), jnp.sin(angle) * sign
    inner = lax.broadcasted_iota(jnp.int32, (BLK, HW), 0).astype(F32) * freq
    cos_i, sin_i = jnp.cos(inner), jnp.sin(inner) * sign

    xk = k_ref[0].astype(F32) + kbias_ref[...]
    kb[0, 0] = (xk * cos + turn(xk) * sin).astype(BF16)
    vb[0, 0] = (v_ref[0].astype(F32) + vbias_ref[...]).astype(BF16)

    pl.semaphore_wait(barrier, len(peers))
    wires = Wires(send_sem, recv_sem)

    lower = range(NZ // 2)
    order = [1, 3, 2][:NZ - 1] if NZ > 2 else [1]
    near, far = near_and_far(NY)

    def arrived(copies):
        for copy in copies:
            copy.wait_recv()

    def hop(buf, k, r):
        last = k == HY
        copies = []
        if not last or r in lower:
            copies.append(wires.start(buf.at[(NY - k + 1) % NY, r], buf.at[NY - k, r], y_peer(1)))
        if not last or r not in lower:
            copies.append(wires.start(buf.at[k - 1, r], buf.at[k, r], y_peer(-1)))
        return copies

    def forward(buf, seen, k, chains):
        for r in chains:
            arrived(seen[k, r])
            seen[k + 1, r] = hop(buf, k + 1, r)

    k_in, v_in = {}, {}
    for r in order:
        k_in[0, r] = [wires.start(kb.at[0, 0], kb.at[0, r], z_peer(NZ - r))]
    k_in[1, 0] = hop(kb, 1, 0)
    g_x = [wires.start(og_hbm, og.at[tp], x_peer(d)) for d in (1, -1)]
    g_z = wires.start(og_hbm, og.at[tp], zl_peer)
    for r in order:
        v_in[0, r] = [wires.start(vb.at[0, 0], vb.at[0, r], z_peer(NZ - r))]
    v_in[1, 0] = hop(vb, 1, 0)
    far_w = wires.start(w_hbm, wb.at[dp], dp_peer)

    for h in range(G):
        cols = slice(h * HW, (h + 1) * HW)
        xq = q_ref[0, :, cols].astype(F32) + qb_ref[cols][None, :]
        rq = xq * cos + turn(xq) * sin
        qn[cols, :] = rq.astype(BF16)
        qt[:, cols] = rq.T.astype(BF16)
    lane = lax.broadcasted_iota(jnp.int32, (1, HW), 1)
    row_pos = jnp.where(lane < BLK, b0 + lane, b1 + (lane - BLK))
    end = jnp.int32(0)
    row_start = jnp.zeros((1, HW), jnp.int32)
    for d in range(doc_ref.shape[1]):
        row_start = jnp.where(row_pos >= end, end, row_start)
        end = end + doc_ref[0, d]
    row_pos = jnp.concatenate([row_pos] * G, axis=1)
    row_start = jnp.concatenate([row_start] * G, axis=1)
    mb[...] = jnp.full(mb.shape, LOW, F32)
    lb[...] = jnp.zeros(lb.shape, F32)
    vs[...] = jnp.zeros(vs.shape, F32)
    acc_o[...] = jnp.zeros(acc_o.shape, F32)
    acc_q[...] = jnp.zeros(acc_q.shape, F32)
    acc_g[...] = jnp.zeros(acc_g.shape, F32)

    def block_row(c, r):
        return lax.rem(z + r, NZ) * NY + lax.rem(y + c, NY)

    def base_step(i, carry):
        for h in range(2):
            bpv[pl.ds(2 * i + h, 1), :] = jnp.full((1, HW), bp_ref[0, h, i] * BLK, jnp.int32)
        return carry

    lax.fori_loop(0, NZ * NY, base_step, 0)

    def over(chunks, body):
        def step(i, carry):
            body(chunks[0] + i * (chunks[-1] - chunks[0]))
            return carry

        lax.fori_loop(0, len(chunks), step, 0)

    def whole(ref, c):
        return ref[c].reshape(ROWS, HW)

    def score(c):
        s = dot(whole(kb, c), qt[...])
        spot = lax.broadcasted_iota(jnp.int32, (BLK, QN), 0)
        most = mb[...]
        for j in range(2 * NZ):
            base = bp_ref[0, j % 2, block_row(c, j // 2)] * BLK
            piece = s[j * BLK:(j + 1) * BLK]
            piece = jnp.where((spot <= row_pos - base) & (spot >= row_start - base), piece, LOW)
            sb[c, j * BLK:(j + 1) * BLK, :] = piece
            most = jnp.maximum(most, jnp.max(piece.reshape(BLK // 8, 8, QN), axis=0))
        mb[...] = most

    def chunks_at(k):
        return [0] if k == 0 else [HY] if k == HY else [k, NY - k]

    w_cols = wb.shape[2]
    left, right = pl.ds(0, w_cols), pl.ds(w_cols, w_cols)

    def opposite(line):
        from_left = zl_line(line) + lax.rem(x + NX - 1, NX)
        from_right = zl_line(line) + lax.rem(x + 1, NX)
        return [
            wires.start(og.at[from_left, :, left], og.at[from_left, :, left], x_peer(1)),
            wires.start(og.at[from_right, :, right], og.at[from_right, :, right], x_peer(-1)),
        ]

    def zl_line(line):
        return (zl if line == 0 else 1 - zl) * NX

    own = [0]
    forward(kb, k_in, 1, own)
    forward(vb, v_in, 1, own)
    forward(kb, k_in, 0, order)
    arrived(g_x)
    g_half = opposite(0)
    if HY > 2:
        forward(kb, k_in, 2, own)
        forward(vb, v_in, 2, own)
    over(chunks_at(0), score)
    g_z.wait_recv()
    partner = zl_line(1) + x
    g_next = [wires.start(og.at[partner], og.at[partner], x_peer(d)) for d in (1, -1)]
    if HY > 3:
        forward(kb, k_in, 3, own)
        forward(vb, v_in, 3, own)
    for k in range(1, HY):
        forward(kb, k_in, k, order)
        over(chunks_at(k), score)
        forward(vb, v_in, k - 1, order)
        if k == 2 or HY == 2:
            arrived(g_next)
            g_last = opposite(1)

    own_g.wait()
    own_w.wait()
    n_inner = w_cols // CHUNK

    def project(half):
        def step(n, carry):
            w = wb[half, :, pl.ds(pl.multiple_of(n * CHUNK, CHUNK), CHUNK)]
            at = pl.multiple_of(half * w_cols + n * CHUNK, CHUNK)
            g = og[:, :, pl.ds(at, CHUNK)].reshape(HW, CHUNK)
            acc_g[...] += lax.dot_general(w, g, NT, preferred_element_type=F32)
            return carry

        lax.fori_loop(0, n_inner, step, 0)

    arrived(g_half)
    arrived(g_last)
    project(dp)
    far_w.wait_recv()
    project(1 - dp)
    for h in range(G):
        dot_t[:, h * HW:(h + 1) * HW] = acc_g[h * HW:(h + 1) * HW, :].astype(BF16)

    for r in range(NZ):
        arrived(k_in[HY, r])
    over(chunks_at(HY), score)

    scale = HW ** -0.5
    top = jnp.max(mb[...], axis=0, keepdims=True) * (scale * LOG2E)

    def soften(c, carry):
        total = lb[...]
        for j in range(2 * NZ):
            rows = slice(j * BLK, (j + 1) * BLK)
            e = jnp.exp2(sb[c, rows, :] * (scale * LOG2E) - top)
            total = total + jnp.sum(e.reshape(BLK // 8, 8, QN), axis=0)
            eb[c, rows, :] = e.astype(BF16)
        lb[...] = total
        return carry

    lax.fori_loop(0, NY, soften, 0)
    inv = 1.0 / jnp.sum(lb[...], axis=0, keepdims=True)
    for h in range(G):
        cols = slice(h * HW, (h + 1) * HW)
        scaled = dot_t[:, cols].astype(F32) * inv[:, cols]
        dot_n[cols, :] = scaled.T.astype(BF16)

    def value_grad(c):
        g = dot(eb[c], dot_n[...])
        vs[...] += jnp.sum(g.reshape(ROWS // 8, 8, HW), axis=0)
        pv[c] = g.astype(BF16).reshape(NZ, HW, HW)

    def attend(c):
        acc_o[...] += lax.dot_general(whole(vb, c), eb[c], TN, preferred_element_type=F32)

    def send_terms(term, r, up, down, k):
        if up:
            term.out[k, r, 0] = wires.start(term.buf.at[HY - k, r], term.slots.at[k, 0, r], y_peer(1))
        if down:
            term.out[k, r, 1] = wires.start(term.buf.at[HY + k, r], term.slots.at[k, 1, r], y_peer(-1))

    def scatter(term, k):
        for r in range(NZ):
            for way, c in ((0, HY - k), (1, HY + k)):
                if (k - 1, r, way) in term.out:
                    term.out[k - 1, r, way].wait_recv()
                    term.buf[c, r] = (term.buf[c, r].astype(F32) + term.slots[k - 1, way, r].astype(F32)).astype(BF16)
            send_terms(term, r, k > 0 or r in lower, k > 0 or r not in lower, k)

    def settle(term):
        for r in order + [0]:
            arrived([term.out[HY - 1, r, way] for way in (0, 1)])
            both = term.slots[HY - 1, 0, r].astype(F32) + term.slots[HY - 1, 1, r].astype(F32)
            term.buf[0, r] = (term.buf[0, r].astype(F32) + both).astype(BF16)
            if r:
                term.last.append(wires.start(term.buf.at[0, r], term.landing.at[r - 1], z_peer(r)))

    def total_of(term):
        arrived(term.last)
        g = term.buf[0, 0].astype(F32)
        for r in range(NZ - 1):
            g = g + term.landing[r].astype(F32)
        return g

    def send_far(term, chunks):
        for c in chunks:
            for r in order[::-1]:
                term.first[c, r] = wires.start(term.buf.at[c, r], term.middle.at[far.index(c), r - 1], z_peer(r))

    def send_near(term, chunks):
        for c in chunks:
            term.direct.append(wires.start(term.buf.at[c], term.slots.at[near.index(c)], y_peer(c)))

    def pass_on(term):
        for c in far:
            g = term.buf[c, 0].astype(F32)
            for r in order[::-1]:
                term.first[c, r].wait_recv()
                g = g + term.middle[far.index(c), r - 1].astype(F32)
            term.buf[c, 0] = g.astype(BF16)
            term.last.append(wires.start(term.buf.at[c, 0], term.far_slots.at[far.index(c)], y_peer(c)))

    def finish_near(term):
        arrived(term.direct)
        for r in order[::-1]:
            g = term.buf[0, r].astype(F32)
            for i in range(len(near)):
                g = g + term.slots[i, r].astype(F32)
            term.buf[0, r] = g.astype(BF16)
            term.last.append(wires.start(term.buf.at[0, r], term.landing.at[r - 1], z_peer(r)))

    def whole_of(term):
        arrived(term.last)
        g = term.buf[0, 0].astype(F32)
        for i in range(len(near)):
            g = g + term.slots[i, 0].astype(F32)
        for i in range(len(far)):
            g = g + term.far_slots[i].astype(F32)
        for r in range(NZ - 1):
            g = g + term.landing[r].astype(F32)
        return g

    v_term, k_term = Term(pv, rv, rv_z), Direct(pk, rk, rk_f, rk_m, rk_z)

    over(chunks_at(HY), value_grad)
    scatter(v_term, 0)
    forward(vb, v_in, HY - 1, order)
    over(chunks_at(HY - 1), value_grad)
    scatter(v_term, 1)
    if HY > 2:
        over(chunks_at(HY - 2), value_grad)
    for k in range(HY):
        over(chunks_at(k), attend)
    if HY > 2:
        scatter(v_term, 2)
    for k in range(1, HY - 2):
        over(chunks_at(k), value_grad)
    for r in range(NZ):
        arrived(v_in[HY, r])
    over(chunks_at(HY), attend)
    o_t = (acc_o[...] * inv).astype(BF16)
    delta = jnp.sum(o_t.astype(F32) * dot_t[...].astype(F32), axis=0, keepdims=True) * inv
    for h in range(G):
        cols = slice(h * HW, (h + 1) * HW)
        o_rows[:, cols] = o_t[:, cols].astype(F32).T.astype(BF16)

    def key_grad(c):
        gp = dot(whole(vb, c), dot_t[...])
        gs = (eb[c].astype(F32) * (gp * inv - delta)).astype(BF16)
        acc_q[...] += lax.dot_general(whole(kb, c), gs, TN, preferred_element_type=F32)
        g = dot(gs, qn[...]) * scale
        pk[c] = g.astype(BF16).reshape(NZ, HW, HW)
        for j in range(2 * NZ):
            t = g[j * BLK:(j + 1) * BLK]
            back = t * cos_i - turn(t) * sin_i
            row = block_row(c, j // 2) * 2 + j % 2
            ub[pl.ds(row, 1), :] = jnp.sum(back, axis=0, keepdims=True)

    for pair in pairs(far):
        over(pair, key_grad)
        send_far(k_term, pair)
    for k in range(3, HY):
        scatter(v_term, k)

    def mix(n, carry):
        half = n // n_inner
        at = pl.multiple_of(lax.rem(n, n_inner) * CHUNK, CHUNK)
        r = dot(o_rows[...], wb[half, :, pl.ds(at, CHUNK)]).astype(BF16)
        to = pl.multiple_of(n * CHUNK, CHUNK)
        po[:, :, :, pl.ds(to, CHUNK)] = r.reshape(NZL, NX, HW // (NZL * NX), CHUNK)
        return carry

    x_far, x_up, x_down = (lax.rem(x + d, NX) for d in (HX, 1, NX - 1))

    lax.fori_loop(0, 2 * n_inner, mix, 0)
    o_far = [
        wires.start(po.at[:, x_far, :, left], rx_half.at[0], x_peer(1)),
        wires.start(po.at[:, x_far, :, right], rx_half.at[1], x_peer(-1)),
    ]
    for pair in pairs(near):
        over(pair, key_grad)
        send_near(k_term, pair)
    over([0], value_grad)
    settle(v_term)
    pass_on(k_term)
    arrived(o_far)
    po[:, x_up, :, left] = (po[:, x_up, :, left].astype(F32) + rx_half[0].astype(F32)).astype(BF16)
    po[:, x_down, :, right] = (po[:, x_down, :, right].astype(F32) + rx_half[1].astype(F32)).astype(BF16)
    o_near = [
        wires.start(po.at[:, x_up], rx_full.at[0], x_peer(1)),
        wires.start(po.at[:, x_down], rx_full.at[1], x_peer(-1)),
    ]
    over([0], key_grad)

    for h in range(G):
        cols = slice(h * HW, (h + 1) * HW)
        g = acc_q[:, cols].T * scale
        g = g * cos - turn(g) * sin
        qg_ref[0, :, cols] = g.astype(BF16)
        btile[0, h:h + 1, :] = jnp.sum(g, axis=0, keepdims=True)
    base_angle = bpv[...].astype(F32) * freq
    u = ub[...]
    u = u * jnp.cos(base_angle) - turn(u) * (jnp.sin(base_angle) * sign)
    btile[0, G:G + 1, :] = jnp.sum(u, axis=0, keepdims=True)
    btile[0, G + 1:G + 2, :] = jnp.sum(vs[...], axis=0, keepdims=True)
    btile[0, G + 2:8, :] = jnp.zeros((8 - G - 2, HW), F32)
    bias_dp = wires.start(btile.at[0], b_dp, dp_peer)

    finish_near(k_term)

    bias_dp.wait_recv()
    btile[1] = btile[0] + b_dp[...]
    bias_z = [wires.start(btile.at[1], b_z.at[r - 1], z_peer(r)) for r in range(1, NZ)]

    arrived(o_near)
    other = 1 - zl
    zs[...] = (
        po[other, x].astype(F32) + rx_full[0, other].astype(F32) + rx_full[1, other].astype(F32)
    ).astype(BF16)
    o_z = wires.start(zs, rz, zl_peer)

    arrived(bias_z)
    total = btile[1]
    for r in range(NZ - 1):
        total = total + b_z[r]
    btile[2] = total
    bias_y = [wires.start(btile.at[2], b_y.at[d - 1], y_peer(d)) for d in range(1, NY)]

    vg_ref[0] = total_of(v_term).astype(BF16)

    o_z.wait_recv()
    out_ref[0] = (
        po[zl, x].astype(F32)
        + rx_full[0, zl].astype(F32)
        + rx_full[1, zl].astype(F32)
        + rz[...].astype(F32)
    ).astype(BF16)

    g = whole_of(k_term)
    kg_ref[0] = (g * cos - turn(g) * sin).astype(BF16)

    arrived(bias_y)
    for d in range(NY - 1):
        total = total + b_y[d]
    bias_ref[...] = total
    wires.finish()


def layer(mesh_shape, q_in, key_input, value_input, q_bias, key_bias, value_bias, out_weight, out_grad, doc_lengths, block_pos):
    NY, NX = mesh_shape["ctx"] // NZ, mesh_shape["tp"] // NZL
    rows, features = q_in.shape[1:]
    G = features // HW
    own_rows, width = out_grad.shape[1:]
    w_cols = out_weight.shape[1]
    QN = G * HW
    ROWS = NZ * HW
    freq = ROPE_BASE ** (-np.arange(0, HW, 2, dtype=np.float64) / HW)
    freq = jnp.asarray(np.concatenate([freq, freq])[None].astype(np.float32))
    vmem, anywhere = pl.BlockSpec(memory_space=pltpu.VMEM), pl.BlockSpec(memory_space=pl.ANY)
    smem = pl.BlockSpec(memory_space=pltpu.SMEM)
    V = pltpu.VMEM
    HY = NY // 2
    ring = [V((HY, 2, NZ, HW, HW), BF16), V((NZ - 1, HW, HW), BF16)]
    near, far = (len(chunks) for chunks in near_and_far(NY))
    direct = [
        V((near, NZ, HW, HW), BF16),
        V((far, HW, HW), BF16),
        V((far, NZ - 1, HW, HW), BF16),
        V((NZ - 1, HW, HW), BF16),
    ]
    copies = 4 * (NZ - 1 + NZ * (2 * HY - 1)) + 16 + NZ + NY
    outs = pl.pallas_call(
        functools.partial(kernel, (NY, NX, G)),
        out_shape=(
            jax.ShapeDtypeStruct((1, own_rows, width), BF16),
            jax.ShapeDtypeStruct((1, rows, features), BF16),
            jax.ShapeDtypeStruct((1, rows, HW), BF16),
            jax.ShapeDtypeStruct((1, rows, HW), BF16),
            jax.ShapeDtypeStruct((8, HW), F32),
        ),
        in_specs=[vmem] * 7 + [smem] * 2 + [anywhere] * 2,
        out_specs=(vmem,) * 5,
        scratch_shapes=[
            V((QN, HW), BF16),
            V((HW, QN), BF16),
            V((NY, NZ, HW, HW), BF16),
            V((NY, NZ, HW, HW), BF16),
            V((NY, ROWS, QN), F32),
            V((NY, ROWS, QN), BF16),
            V((2, features, w_cols), BF16),
            V((NZL * NX, own_rows, width), BF16),
            V((HW, QN), BF16),
            V((QN, HW), BF16),
            V((HW, QN), BF16),
            V((HW, QN), F32),
            V((HW, QN), F32),
            V((QN, HW), F32),
            V((NY, NZ, HW, HW), BF16),
            V((NY, NZ, HW, HW), BF16),
            *direct,
            *ring,
            V((NZL, NX, own_rows, width), BF16),
            V((2, NZL, own_rows, w_cols), BF16),
            V((2, NZL, own_rows, width), BF16),
            V((own_rows, width), BF16),
            V((own_rows, width), BF16),
            V((8, QN), F32),
            V((8, QN), F32),
            V((2 * NZ * NY, HW), F32),
            V((2 * NZ * NY, HW), jnp.int32),
            V((8, HW), F32),
            V((3, 8, HW), F32),
            V((8, HW), F32),
            V((NZ - 1, 8, HW), F32),
            V((NY - 1, 8, HW), F32),
            pltpu.SemaphoreType.DMA((2,)),
            pltpu.SemaphoreType.DMA((copies,)),
            pltpu.SemaphoreType.DMA((copies,)),
        ],
        compiler_params=pltpu.CompilerParams(
            collective_id=0, has_side_effects=True, vmem_limit_bytes=60 * 1024 * 1024
        ),
        name="attention_layer",
    )(
        q_in, key_input, value_input, q_bias, key_bias.reshape(1, -1),
        value_bias.reshape(1, -1), freq, jnp.swapaxes(block_pos, 1, 2), doc_lengths, out_weight, out_grad[0],
    )
    shapes = [jax.ShapeDtypeStruct(o.shape, o.dtype) for o in outs[:4]]
    shapes += [jax.ShapeDtypeStruct((n,), F32) for n in (features, HW, HW)]
    return pl.pallas_call(
        functools.partial(finish, G),
        out_shape=tuple(shapes),
        in_specs=[vmem] * 5,
        out_specs=(vmem,) * 7,
        compiler_params=pltpu.CompilerParams(vmem_limit_bytes=60 * 1024 * 1024),
        name="hand_over",
    )(*outs)


def finish(G, *refs):
    bias_ref, biases = refs[4], refs[9:]
    for source, target in zip(refs[:4], refs[5:9]):
        target[...] = source[...]
    for h in range(G):
        biases[0][h * HW:(h + 1) * HW] = bias_ref[h]
    biases[1][...] = bias_ref[G]
    biases[2][...] = bias_ref[G + 1]


def solution(mesh):
    return jax.shard_map(
        functools.partial(layer, dict(mesh.shape)),
        mesh=mesh,
        in_specs=(
            P("dp", "ctx", "tp"),
            P("dp", "ctx", "tp"),
            P("dp", "ctx", "tp"),
            P("tp"),
            P("tp"),
            P("tp"),
            P("tp", "dp"),
            P("dp", ("ctx", "tp"), None),
            P("dp", None),
            P("dp", None, None),
        ),
        out_specs=(
            P("dp", ("ctx", "tp"), None),
            P("dp", "ctx", "tp"),
            P("dp", "ctx", "tp"),
            P("dp", "ctx", "tp"),
            P("tp"),
            P("tp"),
            P("tp"),
        ),
        check_vma=False,
    )
```

```python
import functools

import jax
import jax.numpy as jnp
import numpy as np
from jax import lax
from jax.experimental import pallas as pl
from jax.experimental.pallas import tpu as pltpu
from jax.sharding import PartitionSpec as P

HW = 128
HALF = HW // 2
BLK = 64
ROPE_BASE = 1000000.0
NZ = 4
NZL = 2
CHUNK = 512
LOW = -1e30
LOG2E = 1.4426950408889634
MESH = pl.DeviceIdType.MESH
F32 = jnp.float32
BF16 = jnp.bfloat16
NT = (((1,), (1,)), ((), ()))
TN = (((0,), (0,)), ((), ()))


def dot(a, b):
    return jnp.dot(a, b, preferred_element_type=F32)


def turn(x):
    return pltpu.roll(x, HALF, 1)


class Wires:
    def __init__(self, send, recv):
        self.send, self.recv, self.all = send, recv, []

    def start(self, src, dst, target):
        n = len(self.all)
        copy = pltpu.make_async_remote_copy(
            src_ref=src,
            dst_ref=dst,
            send_sem=self.send.at[n],
            recv_sem=self.recv.at[n],
            device_id=target,
            device_id_type=MESH,
        )
        copy.start()
        self.all.append(copy)
        return copy

    def finish(self):
        for copy in self.all:
            copy.wait_send()


def near_and_far(n):
    away = [[n // 2]] + [[d, n - d] for d in range(n // 2 - 1, 0, -1)]
    near = [c for pair in away for c in pair if pair[0] <= n // 4]
    return near, [c for pair in away for c in pair if pair[0] > n // 4]


def pairs(chunks):
    odd = len(chunks) % 2
    return [chunks[:1]] * odd + [chunks[i:i + 2] for i in range(odd, len(chunks), 2)]


class Direct:
    def __init__(self, buf, slots, far_slots, middle, landing):
        self.buf, self.slots, self.far_slots = buf, slots, far_slots
        self.middle, self.landing = middle, landing
        self.first, self.direct, self.last = {}, [], []


class Term:
    def __init__(self, buf, slots, landing):
        self.buf, self.slots, self.landing = buf, slots, landing
        self.out, self.last = {}, []


def kernel(
    dims,
    q_ref, k_ref, v_ref, qb_ref, kbias_ref, vbias_ref, freq_ref, bp_ref, doc_ref, w_hbm, og_hbm,
    out_ref, qg_ref, kg_ref, vg_ref, bias_ref,
    qn, qt, kb, vb, sb, eb, wb, og, dot_t, dot_n, o_rows, acc_o, acc_q, acc_g,
    pk, pv, rk, rk_f, rk_m, rk_z, rv, rv_z,
    po, rx_half, rx_full, rz, zs, mb, lb, ub, bpv, vs, btile, b_dp, b_z, b_y,
    local_sem, send_sem, recv_sem,
):
    NY, NX, G = dims
    ctx, tp, dp = lax.axis_index("ctx"), lax.axis_index("tp"), lax.axis_index("dp")
    z, y = ctx // NY, lax.rem(ctx, NY)
    zl, x = tp // NX, lax.rem(tp, NX)
    HY, HX = NY // 2, NX // 2
    QN = G * HW
    ROWS = NZ * HW

    def y_peer(d):
        return {"ctx": z * NY + lax.rem(y + d + NY, NY)}

    def z_peer(d):
        return {"ctx": lax.rem(z + d, NZ) * NY + y}

    def x_peer(d):
        return {"tp": zl * NX + lax.rem(x + d + NX, NX)}

    zl_peer = {"tp": (1 - zl) * NX + x}
    dp_peer = {"dp": 1 - dp}

    barrier = pltpu.get_barrier_semaphore()
    peers = [y_peer(d) for d in range(1, NY)] + [z_peer(d) for d in range(1, NZ)]
    peers += [x_peer(1), x_peer(-1), zl_peer, dp_peer]
    for peer in peers:
        pl.semaphore_signal(barrier, inc=1, device_id=peer, device_id_type=MESH)

    own_w = pltpu.make_async_copy(w_hbm, wb.at[dp], local_sem.at[0])
    own_w.start()
    own_g = pltpu.make_async_copy(og_hbm, og.at[tp], local_sem.at[1])
    own_g.start()

    b0, b1 = bp_ref[0, 0, ctx] * BLK, bp_ref[0, 1, ctx] * BLK
    sub = lax.broadcasted_iota(jnp.int32, (HW, HW), 0)
    pos = jnp.where(sub < BLK, b0 + sub, b1 + (sub - BLK))
    freq = freq_ref[...]
    angle = pos.astype(F32) * freq
    sign = jnp.where(lax.broadcasted_iota(jnp.int32, (1, HW), 1) < HALF, -1.0, 1.0)
    cos, sin = jnp.cos(angle), jnp.sin(angle) * sign
    inner = lax.broadcasted_iota(jnp.int32, (BLK, HW), 0).astype(F32) * freq
    cos_i, sin_i = jnp.cos(inner), jnp.sin(inner) * sign

    xk = k_ref[0].astype(F32) + kbias_ref[...]
    kb[0, 0] = (xk * cos + turn(xk) * sin).astype(BF16)
    vb[0, 0] = (v_ref[0].astype(F32) + vbias_ref[...]).astype(BF16)

    pl.semaphore_wait(barrier, len(peers))
    wires = Wires(send_sem, recv_sem)

    lower = range(NZ // 2)
    order = [1, 3, 2][:NZ - 1] if NZ > 2 else [1]
    near, far = near_and_far(NY)

    def arrived(copies):
        for copy in copies:
            copy.wait_recv()

    def hop(buf, k, r):
        last = k == HY
        copies = []
        if not last or r in lower:
            copies.append(wires.start(buf.at[(NY - k + 1) % NY, r], buf.at[NY - k, r], y_peer(1)))
        if not last or r not in lower:
            copies.append(wires.start(buf.at[k - 1, r], buf.at[k, r], y_peer(-1)))
        return copies

    def forward(buf, seen, k, chains):
        for r in chains:
            arrived(seen[k, r])
            seen[k + 1, r] = hop(buf, k + 1, r)

    k_in, v_in = {}, {}
    for r in order:
        k_in[0, r] = [wires.start(kb.at[0, 0], kb.at[0, r], z_peer(NZ - r))]
    k_in[1, 0] = hop(kb, 1, 0)
    g_x = [wires.start(og_hbm, og.at[tp], x_peer(d)) for d in (1, -1)]
    g_z = wires.start(og_hbm, og.at[tp], zl_peer)
    for r in order:
        v_in[0, r] = [wires.start(vb.at[0, 0], vb.at[0, r], z_peer(NZ - r))]
    v_in[1, 0] = hop(vb, 1, 0)
    far_w = wires.start(w_hbm, wb.at[dp], dp_peer)

    for h in range(G):
        cols = slice(h * HW, (h + 1) * HW)
        xq = q_ref[0, :, cols].astype(F32) + qb_ref[cols][None, :]
        rq = xq * cos + turn(xq) * sin
        qn[cols, :] = rq.astype(BF16)
        qt[:, cols] = rq.T.astype(BF16)
    lane = lax.broadcasted_iota(jnp.int32, (1, HW), 1)
    row_pos = jnp.where(lane < BLK, b0 + lane, b1 + (lane - BLK))
    end = jnp.int32(0)
    row_start = jnp.zeros((1, HW), jnp.int32)
    for d in range(doc_ref.shape[1]):
        row_start = jnp.where(row_pos >= end, end, row_start)
        end = end + doc_ref[0, d]
    row_pos = jnp.concatenate([row_pos] * G, axis=1)
    row_start = jnp.concatenate([row_start] * G, axis=1)
    mb[...] = jnp.full(mb.shape, LOW, F32)
    lb[...] = jnp.zeros(lb.shape, F32)
    vs[...] = jnp.zeros(vs.shape, F32)
    acc_o[...] = jnp.zeros(acc_o.shape, F32)
    acc_q[...] = jnp.zeros(acc_q.shape, F32)
    acc_g[...] = jnp.zeros(acc_g.shape, F32)

    def block_row(c, r):
        return lax.rem(z + r, NZ) * NY + lax.rem(y + c, NY)

    def base_step(i, carry):
        for h in range(2):
            bpv[pl.ds(2 * i + h, 1), :] = jnp.full((1, HW), bp_ref[0, h, i] * BLK, jnp.int32)
        return carry

    lax.fori_loop(0, NZ * NY, base_step, 0)

    def over(chunks, body):
        def step(i, carry):
            body(chunks[0] + i * (chunks[-1] - chunks[0]))
            return carry

        lax.fori_loop(0, len(chunks), step, 0)

    def whole(ref, c):
        return ref[c].reshape(ROWS, HW)

    def score(c):
        s = dot(whole(kb, c), qt[...])
        spot = lax.broadcasted_iota(jnp.int32, (BLK, QN), 0)
        most = mb[...]
        for j in range(2 * NZ):
            base = bp_ref[0, j % 2, block_row(c, j // 2)] * BLK
            piece = s[j * BLK:(j + 1) * BLK]
            piece = jnp.where((spot <= row_pos - base) & (spot >= row_start - base), piece, LOW)
            sb[c, j * BLK:(j + 1) * BLK, :] = piece
            most = jnp.maximum(most, jnp.max(piece.reshape(BLK // 8, 8, QN), axis=0))
        mb[...] = most

    def chunks_at(k):
        return [0] if k == 0 else [HY] if k == HY else [k, NY - k]

    w_cols = wb.shape[2]
    left, right = pl.ds(0, w_cols), pl.ds(w_cols, w_cols)

    def opposite(line):
        from_left = zl_line(line) + lax.rem(x + NX - 1, NX)
        from_right = zl_line(line) + lax.rem(x + 1, NX)
        return [
            wires.start(og.at[from_left, :, left], og.at[from_left, :, left], x_peer(1)),
            wires.start(og.at[from_right, :, right], og.at[from_right, :, right], x_peer(-1)),
        ]

    def zl_line(line):
        return (zl if line == 0 else 1 - zl) * NX

    own = [0]
    forward(kb, k_in, 1, own)
    forward(vb, v_in, 1, own)
    forward(kb, k_in, 0, order)
    arrived(g_x)
    g_half = opposite(0)
    if HY > 2:
        forward(kb, k_in, 2, own)
        forward(vb, v_in, 2, own)
    over(chunks_at(0), score)
    g_z.wait_recv()
    partner = zl_line(1) + x
    g_next = [wires.start(og.at[partner], og.at[partner], x_peer(d)) for d in (1, -1)]
    if HY > 3:
        forward(kb, k_in, 3, own)
        forward(vb, v_in, 3, own)
    for k in range(1, HY):
        forward(kb, k_in, k, order)
        over(chunks_at(k), score)
        forward(vb, v_in, k - 1, order)
        if k == 2 or HY == 2:
            arrived(g_next)
            g_last = opposite(1)

    own_g.wait()
    own_w.wait()
    n_inner = w_cols // CHUNK

    def project(half):
        def step(n, carry):
            w = wb[half, :, pl.ds(pl.multiple_of(n * CHUNK, CHUNK), CHUNK)]
            at = pl.multiple_of(half * w_cols + n * CHUNK, CHUNK)
            g = og[:, :, pl.ds(at, CHUNK)].reshape(HW, CHUNK)
            acc_g[...] += lax.dot_general(w, g, NT, preferred_element_type=F32)
            return carry

        lax.fori_loop(0, n_inner, step, 0)

    arrived(g_half)
    arrived(g_last)
    project(dp)
    far_w.wait_recv()
    project(1 - dp)
    for h in range(G):
        dot_t[:, h * HW:(h + 1) * HW] = acc_g[h * HW:(h + 1) * HW, :].astype(BF16)

    for r in range(NZ):
        arrived(k_in[HY, r])
    over(chunks_at(HY), score)

    scale = HW ** -0.5
    top = jnp.max(mb[...], axis=0, keepdims=True) * (scale * LOG2E)

    def soften(c, carry):
        total = lb[...]
        for j in range(2 * NZ):
            rows = slice(j * BLK, (j + 1) * BLK)
            e = jnp.exp2(sb[c, rows, :] * (scale * LOG2E) - top)
            total = total + jnp.sum(e.reshape(BLK // 8, 8, QN), axis=0)
            eb[c, rows, :] = e.astype(BF16)
        lb[...] = total
        return carry

    lax.fori_loop(0, NY, soften, 0)
    inv = 1.0 / jnp.sum(lb[...], axis=0, keepdims=True)
    for h in range(G):
        cols = slice(h * HW, (h + 1) * HW)
        scaled = dot_t[:, cols].astype(F32) * inv[:, cols]
        dot_n[cols, :] = scaled.T.astype(BF16)

    def value_grad(c):
        g = dot(eb[c], dot_n[...])
        vs[...] += jnp.sum(g.reshape(ROWS // 8, 8, HW), axis=0)
        pv[c] = g.astype(BF16).reshape(NZ, HW, HW)

    def attend(c):
        acc_o[...] += lax.dot_general(whole(vb, c), eb[c], TN, preferred_element_type=F32)

    def send_terms(term, r, up, down, k):
        if up:
            term.out[k, r, 0] = wires.start(term.buf.at[HY - k, r], term.slots.at[k, 0, r], y_peer(1))
        if down:
            term.out[k, r, 1] = wires.start(term.buf.at[HY + k, r], term.slots.at[k, 1, r], y_peer(-1))

    def scatter(term, k):
        for r in range(NZ):
            for way, c in ((0, HY - k), (1, HY + k)):
                if (k - 1, r, way) in term.out:
                    term.out[k - 1, r, way].wait_recv()
                    term.buf[c, r] = (term.buf[c, r].astype(F32) + term.slots[k - 1, way, r].astype(F32)).astype(BF16)
            send_terms(term, r, k > 0 or r in lower, k > 0 or r not in lower, k)

    def settle(term):
        for r in order + [0]:
            arrived([term.out[HY - 1, r, way] for way in (0, 1)])
            both = term.slots[HY - 1, 0, r].astype(F32) + term.slots[HY - 1, 1, r].astype(F32)
            term.buf[0, r] = (term.buf[0, r].astype(F32) + both).astype(BF16)
            if r:
                term.last.append(wires.start(term.buf.at[0, r], term.landing.at[r - 1], z_peer(r)))

    def total_of(term):
        arrived(term.last)
        g = term.buf[0, 0].astype(F32)
        for r in range(NZ - 1):
            g = g + term.landing[r].astype(F32)
        return g

    def send_far(term, chunks):
        for c in chunks:
            for r in order[::-1]:
                term.first[c, r] = wires.start(term.buf.at[c, r], term.middle.at[far.index(c), r - 1], z_peer(r))

    def send_near(term, chunks):
        for c in chunks:
            term.direct.append(wires.start(term.buf.at[c], term.slots.at[near.index(c)], y_peer(c)))

    def pass_on(term):
        for c in far:
            g = term.buf[c, 0].astype(F32)
            for r in order[::-1]:
                term.first[c, r].wait_recv()
                g = g + term.middle[far.index(c), r - 1].astype(F32)
            term.buf[c, 0] = g.astype(BF16)
            term.last.append(wires.start(term.buf.at[c, 0], term.far_slots.at[far.index(c)], y_peer(c)))

    def finish_near(term):
        arrived(term.direct)
        for r in order[::-1]:
            g = term.buf[0, r].astype(F32)
            for i in range(len(near)):
                g = g + term.slots[i, r].astype(F32)
            term.buf[0, r] = g.astype(BF16)
            term.last.append(wires.start(term.buf.at[0, r], term.landing.at[r - 1], z_peer(r)))

    def whole_of(term):
        arrived(term.last)
        g = term.buf[0, 0].astype(F32)
        for i in range(len(near)):
            g = g + term.slots[i, 0].astype(F32)
        for i in range(len(far)):
            g = g + term.far_slots[i].astype(F32)
        for r in range(NZ - 1):
            g = g + term.landing[r].astype(F32)
        return g

    v_term, k_term = Term(pv, rv, rv_z), Direct(pk, rk, rk_f, rk_m, rk_z)

    over(chunks_at(HY), value_grad)
    scatter(v_term, 0)
    forward(vb, v_in, HY - 1, order)
    over(chunks_at(HY - 1), value_grad)
    scatter(v_term, 1)
    if HY > 2:
        over(chunks_at(HY - 2), value_grad)
    for k in range(HY):
        over(chunks_at(k), attend)
    if HY > 2:
        scatter(v_term, 2)
    for k in range(1, HY - 2):
        over(chunks_at(k), value_grad)
    for r in range(NZ):
        arrived(v_in[HY, r])
    over(chunks_at(HY), attend)
    o_t = (acc_o[...] * inv).astype(BF16)
    delta = jnp.sum(o_t.astype(F32) * dot_t[...].astype(F32), axis=0, keepdims=True) * inv
    for h in range(G):
        cols = slice(h * HW, (h + 1) * HW)
        o_rows[:, cols] = o_t[:, cols].astype(F32).T.astype(BF16)

    def key_grad(c):
        gp = dot(whole(vb, c), dot_t[...])
        gs = (eb[c].astype(F32) * (gp * inv - delta)).astype(BF16)
        acc_q[...] += lax.dot_general(whole(kb, c), gs, TN, preferred_element_type=F32)
        g = dot(gs, qn[...]) * scale
        pk[c] = g.astype(BF16).reshape(NZ, HW, HW)
        for j in range(2 * NZ):
            t = g[j * BLK:(j + 1) * BLK]
            back = t * cos_i - turn(t) * sin_i
            row = block_row(c, j // 2) * 2 + j % 2
            ub[pl.ds(row, 1), :] = jnp.sum(back, axis=0, keepdims=True)

    def mix(n, carry):
        half = n // n_inner
        at = pl.multiple_of(lax.rem(n, n_inner) * CHUNK, CHUNK)
        r = dot(o_rows[...], wb[half, :, pl.ds(at, CHUNK)]).astype(BF16)
        to = pl.multiple_of(n * CHUNK, CHUNK)
        po[:, :, :, pl.ds(to, CHUNK)] = r.reshape(NZL, NX, HW // (NZL * NX), CHUNK)
        return carry

    x_far, x_up, x_down = (lax.rem(x + d, NX) for d in (HX, 1, NX - 1))

    lax.fori_loop(0, 2 * n_inner, mix, 0)
    o_far = [
        wires.start(po.at[:, x_far, :, left], rx_half.at[0], x_peer(1)),
        wires.start(po.at[:, x_far, :, right], rx_half.at[1], x_peer(-1)),
    ]
    o_near = [
        wires.start(po.at[:, x_up, :, right], rx_full.at[0, :, :, right], x_peer(1)),
        wires.start(po.at[:, x_down, :, left], rx_full.at[1, :, :, left], x_peer(-1)),
    ]
    for pair in pairs(far):
        over(pair, key_grad)
        send_far(k_term, pair)
    for k in range(3, HY):
        scatter(v_term, k)

    for pair in pairs(near):
        over(pair, key_grad)
        send_near(k_term, pair)
    arrived(o_far)
    po[:, x_up, :, left] = (po[:, x_up, :, left].astype(F32) + rx_half[0].astype(F32)).astype(BF16)
    po[:, x_down, :, right] = (po[:, x_down, :, right].astype(F32) + rx_half[1].astype(F32)).astype(BF16)
    o_near += [
        wires.start(po.at[:, x_up, :, left], rx_full.at[0, :, :, left], x_peer(1)),
        wires.start(po.at[:, x_down, :, right], rx_full.at[1, :, :, right], x_peer(-1)),
    ]
    over([0], key_grad)
    over([0], value_grad)
    settle(v_term)
    pass_on(k_term)

    for h in range(G):
        cols = slice(h * HW, (h + 1) * HW)
        g = acc_q[:, cols].T * scale
        g = g * cos - turn(g) * sin
        qg_ref[0, :, cols] = g.astype(BF16)
        btile[0, h:h + 1, :] = jnp.sum(g, axis=0, keepdims=True)
    base_angle = bpv[...].astype(F32) * freq
    u = ub[...]
    u = u * jnp.cos(base_angle) - turn(u) * (jnp.sin(base_angle) * sign)
    btile[0, G:G + 1, :] = jnp.sum(u, axis=0, keepdims=True)
    btile[0, G + 1:G + 2, :] = jnp.sum(vs[...], axis=0, keepdims=True)
    btile[0, G + 2:8, :] = jnp.zeros((8 - G - 2, HW), F32)
    bias_dp = wires.start(btile.at[0], b_dp, dp_peer)

    finish_near(k_term)

    bias_dp.wait_recv()
    btile[1] = btile[0] + b_dp[...]
    bias_z = [wires.start(btile.at[1], b_z.at[r - 1], z_peer(r)) for r in range(1, NZ)]

    arrived(o_near)
    other = 1 - zl
    zs[...] = (
        po[other, x].astype(F32) + rx_full[0, other].astype(F32) + rx_full[1, other].astype(F32)
    ).astype(BF16)
    o_z = wires.start(zs, rz, zl_peer)

    arrived(bias_z)
    total = btile[1]
    for r in range(NZ - 1):
        total = total + b_z[r]
    btile[2] = total
    bias_y = [wires.start(btile.at[2], b_y.at[d - 1], y_peer(d)) for d in range(1, NY)]

    vg_ref[0] = total_of(v_term).astype(BF16)

    o_z.wait_recv()
    out_ref[0] = (
        po[zl, x].astype(F32)
        + rx_full[0, zl].astype(F32)
        + rx_full[1, zl].astype(F32)
        + rz[...].astype(F32)
    ).astype(BF16)

    g = whole_of(k_term)
    kg_ref[0] = (g * cos - turn(g) * sin).astype(BF16)

    arrived(bias_y)
    for d in range(NY - 1):
        total = total + b_y[d]
    bias_ref[...] = total
    wires.finish()


def layer(mesh_shape, q_in, key_input, value_input, q_bias, key_bias, value_bias, out_weight, out_grad, doc_lengths, block_pos):
    NY, NX = mesh_shape["ctx"] // NZ, mesh_shape["tp"] // NZL
    rows, features = q_in.shape[1:]
    G = features // HW
    own_rows, width = out_grad.shape[1:]
    w_cols = out_weight.shape[1]
    QN = G * HW
    ROWS = NZ * HW
    freq = ROPE_BASE ** (-np.arange(0, HW, 2, dtype=np.float64) / HW)
    freq = jnp.asarray(np.concatenate([freq, freq])[None].astype(np.float32))
    vmem, anywhere = pl.BlockSpec(memory_space=pltpu.VMEM), pl.BlockSpec(memory_space=pl.ANY)
    smem = pl.BlockSpec(memory_space=pltpu.SMEM)
    V = pltpu.VMEM
    HY = NY // 2
    ring = [V((HY, 2, NZ, HW, HW), BF16), V((NZ - 1, HW, HW), BF16)]
    near, far = (len(chunks) for chunks in near_and_far(NY))
    direct = [
        V((near, NZ, HW, HW), BF16),
        V((far, HW, HW), BF16),
        V((far, NZ - 1, HW, HW), BF16),
        V((NZ - 1, HW, HW), BF16),
    ]
    copies = 4 * (NZ - 1 + NZ * (2 * HY - 1)) + 16 + NZ + NY
    outs = pl.pallas_call(
        functools.partial(kernel, (NY, NX, G)),
        out_shape=(
            jax.ShapeDtypeStruct((1, own_rows, width), BF16),
            jax.ShapeDtypeStruct((1, rows, features), BF16),
            jax.ShapeDtypeStruct((1, rows, HW), BF16),
            jax.ShapeDtypeStruct((1, rows, HW), BF16),
            jax.ShapeDtypeStruct((8, HW), F32),
        ),
        in_specs=[vmem] * 7 + [smem] * 2 + [anywhere] * 2,
        out_specs=(vmem,) * 5,
        scratch_shapes=[
            V((QN, HW), BF16),
            V((HW, QN), BF16),
            V((NY, NZ, HW, HW), BF16),
            V((NY, NZ, HW, HW), BF16),
            V((NY, ROWS, QN), F32),
            V((NY, ROWS, QN), BF16),
            V((2, features, w_cols), BF16),
            V((NZL * NX, own_rows, width), BF16),
            V((HW, QN), BF16),
            V((QN, HW), BF16),
            V((HW, QN), BF16),
            V((HW, QN), F32),
            V((HW, QN), F32),
            V((QN, HW), F32),
            V((NY, NZ, HW, HW), BF16),
            V((NY, NZ, HW, HW), BF16),
            *direct,
            *ring,
            V((NZL, NX, own_rows, width), BF16),
            V((2, NZL, own_rows, w_cols), BF16),
            V((2, NZL, own_rows, width), BF16),
            V((own_rows, width), BF16),
            V((own_rows, width), BF16),
            V((8, QN), F32),
            V((8, QN), F32),
            V((2 * NZ * NY, HW), F32),
            V((2 * NZ * NY, HW), jnp.int32),
            V((8, HW), F32),
            V((3, 8, HW), F32),
            V((8, HW), F32),
            V((NZ - 1, 8, HW), F32),
            V((NY - 1, 8, HW), F32),
            pltpu.SemaphoreType.DMA((2,)),
            pltpu.SemaphoreType.DMA((copies,)),
            pltpu.SemaphoreType.DMA((copies,)),
        ],
        compiler_params=pltpu.CompilerParams(
            collective_id=0, has_side_effects=True, vmem_limit_bytes=60 * 1024 * 1024
        ),
        name="attention_layer",
    )(
        q_in, key_input, value_input, q_bias, key_bias.reshape(1, -1),
        value_bias.reshape(1, -1), freq, jnp.swapaxes(block_pos, 1, 2), doc_lengths, out_weight, out_grad[0],
    )
    shapes = [jax.ShapeDtypeStruct(o.shape, o.dtype) for o in outs[:4]]
    shapes += [jax.ShapeDtypeStruct((n,), F32) for n in (features, HW, HW)]
    return pl.pallas_call(
        functools.partial(finish, G),
        out_shape=tuple(shapes),
        in_specs=[vmem] * 5,
        out_specs=(vmem,) * 7,
        compiler_params=pltpu.CompilerParams(vmem_limit_bytes=60 * 1024 * 1024),
        name="hand_over",
    )(*outs)


def finish(G, *refs):
    bias_ref, biases = refs[4], refs[9:]
    for source, target in zip(refs[:4], refs[5:9]):
        target[...] = source[...]
    for h in range(G):
        biases[0][h * HW:(h + 1) * HW] = bias_ref[h]
    biases[1][...] = bias_ref[G]
    biases[2][...] = bias_ref[G + 1]


def solution(mesh):
    return jax.shard_map(
        functools.partial(layer, dict(mesh.shape)),
        mesh=mesh,
        in_specs=(
            P("dp", "ctx", "tp"),
            P("dp", "ctx", "tp"),
            P("dp", "ctx", "tp"),
            P("tp"),
            P("tp"),
            P("tp"),
            P("tp", "dp"),
            P("dp", ("ctx", "tp"), None),
            P("dp", None),
            P("dp", None, None),
        ),
        out_specs=(
            P("dp", ("ctx", "tp"), None),
            P("dp", "ctx", "tp"),
            P("dp", "ctx", "tp"),
            P("dp", "ctx", "tp"),
            P("tp"),
            P("tp"),
            P("tp"),
        ),
        check_vma=False,
    )
```

```python
import functools

import jax
import jax.numpy as jnp
import numpy as np
from jax import lax
from jax.experimental import pallas as pl
from jax.experimental.pallas import tpu as pltpu
from jax.sharding import PartitionSpec as P

HW = 128
HALF = HW // 2
BLK = 64
ROPE_BASE = 1000000.0
NZ = 4
NZL = 2
CHUNK = 512
LOW = -1e30
LOG2E = 1.4426950408889634
MESH = pl.DeviceIdType.MESH
F32 = jnp.float32
BF16 = jnp.bfloat16
NT = (((1,), (1,)), ((), ()))
TN = (((0,), (0,)), ((), ()))


def dot(a, b):
    return jnp.dot(a, b, preferred_element_type=F32)


def turn(x):
    return pltpu.roll(x, HALF, 1)


class Wires:
    def __init__(self, send, recv):
        self.send, self.recv, self.all = send, recv, []

    def start(self, src, dst, target):
        n = len(self.all)
        copy = pltpu.make_async_remote_copy(
            src_ref=src,
            dst_ref=dst,
            send_sem=self.send.at[n],
            recv_sem=self.recv.at[n],
            device_id=target,
            device_id_type=MESH,
        )
        copy.start()
        self.all.append(copy)
        return copy

    def finish(self):
        for copy in self.all:
            copy.wait_send()


def near_and_far(n):
    away = [[n // 2]] + [[d, n - d] for d in range(n // 2 - 1, 0, -1)]
    near = [c for pair in away for c in pair if pair[0] <= n // 4]
    return near, [c for pair in away for c in pair if pair[0] > n // 4]


def pairs(chunks):
    odd = len(chunks) % 2
    return [chunks[:1]] * odd + [chunks[i:i + 2] for i in range(odd, len(chunks), 2)]


class Direct:
    def __init__(self, buf, slots, far_slots, middle, landing):
        self.buf, self.slots, self.far_slots = buf, slots, far_slots
        self.middle, self.landing = middle, landing
        self.first, self.direct, self.last = {}, [], []


class Term:
    def __init__(self, buf, slots, landing):
        self.buf, self.slots, self.landing = buf, slots, landing
        self.out, self.last = {}, []


def kernel(
    dims,
    q_ref, k_ref, v_ref, qb_ref, kbias_ref, vbias_ref, freq_ref, bp_ref, doc_ref, w_hbm, og_hbm,
    out_ref, qg_ref, kg_ref, vg_ref, bias_ref,
    qn, qt, kb, vb, sb, eb, wb, og, dot_t, dot_n, o_rows, acc_o, acc_q, acc_g,
    pk, pv, rk, rk_f, rk_m, rk_z, rv, rv_f, rv_m, rv_z,
    po, rx_half, rx_full, rz, zs, mb, lb, ub, bpv, vs, btile, b_dp, b_z, b_y,
    local_sem, send_sem, recv_sem,
):
    NY, NX, G = dims
    ctx, tp, dp = lax.axis_index("ctx"), lax.axis_index("tp"), lax.axis_index("dp")
    z, y = ctx // NY, lax.rem(ctx, NY)
    zl, x = tp // NX, lax.rem(tp, NX)
    HY, HX = NY // 2, NX // 2
    QN = G * HW
    ROWS = NZ * HW

    def y_peer(d):
        return {"ctx": z * NY + lax.rem(y + d + NY, NY)}

    def z_peer(d):
        return {"ctx": lax.rem(z + d, NZ) * NY + y}

    def x_peer(d):
        return {"tp": zl * NX + lax.rem(x + d + NX, NX)}

    zl_peer = {"tp": (1 - zl) * NX + x}
    dp_peer = {"dp": 1 - dp}

    barrier = pltpu.get_barrier_semaphore()
    peers = [y_peer(d) for d in range(1, NY)] + [z_peer(d) for d in range(1, NZ)]
    peers += [x_peer(1), x_peer(-1), zl_peer, dp_peer]
    for peer in peers:
        pl.semaphore_signal(barrier, inc=1, device_id=peer, device_id_type=MESH)

    own_w = pltpu.make_async_copy(w_hbm, wb.at[dp], local_sem.at[0])
    own_w.start()
    own_g = pltpu.make_async_copy(og_hbm, og.at[tp], local_sem.at[1])
    own_g.start()

    b0, b1 = bp_ref[0, 0, ctx] * BLK, bp_ref[0, 1, ctx] * BLK
    sub = lax.broadcasted_iota(jnp.int32, (HW, HW), 0)
    pos = jnp.where(sub < BLK, b0 + sub, b1 + (sub - BLK))
    freq = freq_ref[...]
    angle = pos.astype(F32) * freq
    sign = jnp.where(lax.broadcasted_iota(jnp.int32, (1, HW), 1) < HALF, -1.0, 1.0)
    cos, sin = jnp.cos(angle), jnp.sin(angle) * sign
    inner = lax.broadcasted_iota(jnp.int32, (BLK, HW), 0).astype(F32) * freq
    cos_i, sin_i = jnp.cos(inner), jnp.sin(inner) * sign

    xk = k_ref[0].astype(F32) + kbias_ref[...]
    kb[0, 0] = (xk * cos + turn(xk) * sin).astype(BF16)
    vb[0, 0] = (v_ref[0].astype(F32) + vbias_ref[...]).astype(BF16)

    pl.semaphore_wait(barrier, len(peers))
    wires = Wires(send_sem, recv_sem)

    lower = range(NZ // 2)
    order = [1, 3, 2][:NZ - 1] if NZ > 2 else [1]
    near, far = near_and_far(NY)

    def arrived(copies):
        for copy in copies:
            copy.wait_recv()

    def hop(buf, k, r):
        last = k == HY
        copies = []
        if not last or r in lower:
            copies.append(wires.start(buf.at[(NY - k + 1) % NY, r], buf.at[NY - k, r], y_peer(1)))
        if not last or r not in lower:
            copies.append(wires.start(buf.at[k - 1, r], buf.at[k, r], y_peer(-1)))
        return copies

    def forward(buf, seen, k, chains):
        for r in chains:
            arrived(seen[k, r])
            seen[k + 1, r] = hop(buf, k + 1, r)

    k_in, v_in = {}, {}
    for r in order:
        k_in[0, r] = [wires.start(kb.at[0, 0], kb.at[0, r], z_peer(NZ - r))]
    k_in[1, 0] = hop(kb, 1, 0)
    g_x = [wires.start(og_hbm, og.at[tp], x_peer(d)) for d in (1, -1)]
    g_z = wires.start(og_hbm, og.at[tp], zl_peer)
    for r in order:
        v_in[0, r] = [wires.start(vb.at[0, 0], vb.at[0, r], z_peer(NZ - r))]
    v_in[1, 0] = hop(vb, 1, 0)
    far_w = wires.start(w_hbm, wb.at[dp], dp_peer)

    for h in range(G):
        cols = slice(h * HW, (h + 1) * HW)
        xq = q_ref[0, :, cols].astype(F32) + qb_ref[cols][None, :]
        rq = xq * cos + turn(xq) * sin
        qn[cols, :] = rq.astype(BF16)
        qt[:, cols] = rq.T.astype(BF16)
    lane = lax.broadcasted_iota(jnp.int32, (1, HW), 1)
    row_pos = jnp.where(lane < BLK, b0 + lane, b1 + (lane - BLK))
    end = jnp.int32(0)
    row_start = jnp.zeros((1, HW), jnp.int32)
    for d in range(doc_ref.shape[1]):
        row_start = jnp.where(row_pos >= end, end, row_start)
        end = end + doc_ref[0, d]
    row_pos = jnp.concatenate([row_pos] * G, axis=1)
    row_start = jnp.concatenate([row_start] * G, axis=1)
    mb[...] = jnp.full(mb.shape, LOW, F32)
    lb[...] = jnp.zeros(lb.shape, F32)
    vs[...] = jnp.zeros(vs.shape, F32)
    acc_o[...] = jnp.zeros(acc_o.shape, F32)
    acc_q[...] = jnp.zeros(acc_q.shape, F32)
    acc_g[...] = jnp.zeros(acc_g.shape, F32)

    def block_row(c, r):
        return lax.rem(z + r, NZ) * NY + lax.rem(y + c, NY)

    def base_step(i, carry):
        for h in range(2):
            bpv[pl.ds(2 * i + h, 1), :] = jnp.full((1, HW), bp_ref[0, h, i] * BLK, jnp.int32)
        return carry

    lax.fori_loop(0, NZ * NY, base_step, 0)

    def over(chunks, body):
        def step(i, carry):
            body(chunks[0] + i * (chunks[-1] - chunks[0]))
            return carry

        lax.fori_loop(0, len(chunks), step, 0)

    def whole(ref, c):
        return ref[c].reshape(ROWS, HW)

    def score(c):
        s = dot(whole(kb, c), qt[...])
        spot = lax.broadcasted_iota(jnp.int32, (BLK, QN), 0)
        most = mb[...]
        for j in range(2 * NZ):
            base = bp_ref[0, j % 2, block_row(c, j // 2)] * BLK
            piece = s[j * BLK:(j + 1) * BLK]
            piece = jnp.where((spot <= row_pos - base) & (spot >= row_start - base), piece, LOW)
            sb[c, j * BLK:(j + 1) * BLK, :] = piece
            most = jnp.maximum(most, jnp.max(piece.reshape(BLK // 8, 8, QN), axis=0))
        mb[...] = most

    def chunks_at(k):
        return [0] if k == 0 else [HY] if k == HY else [k, NY - k]

    w_cols = wb.shape[2]
    left, right = pl.ds(0, w_cols), pl.ds(w_cols, w_cols)

    def opposite(line):
        from_left = zl_line(line) + lax.rem(x + NX - 1, NX)
        from_right = zl_line(line) + lax.rem(x + 1, NX)
        return [
            wires.start(og.at[from_left, :, left], og.at[from_left, :, left], x_peer(1)),
            wires.start(og.at[from_right, :, right], og.at[from_right, :, right], x_peer(-1)),
        ]

    def zl_line(line):
        return (zl if line == 0 else 1 - zl) * NX

    own = [0]
    forward(kb, k_in, 1, own)
    forward(vb, v_in, 1, own)
    forward(kb, k_in, 0, order)
    arrived(g_x)
    g_half = opposite(0)
    if HY > 2:
        forward(kb, k_in, 2, own)
        forward(vb, v_in, 2, own)
    over(chunks_at(0), score)
    g_z.wait_recv()
    partner = zl_line(1) + x
    g_next = [wires.start(og.at[partner], og.at[partner], x_peer(d)) for d in (1, -1)]
    if HY > 3:
        forward(kb, k_in, 3, own)
        forward(vb, v_in, 3, own)
    for k in range(1, HY):
        forward(kb, k_in, k, order)
        over(chunks_at(k), score)
        forward(vb, v_in, k - 1, order)
        if k == 2 or HY == 2:
            arrived(g_next)
            g_last = opposite(1)

    own_g.wait()
    own_w.wait()
    n_inner = w_cols // CHUNK

    def project(half):
        def step(n, carry):
            w = wb[half, :, pl.ds(pl.multiple_of(n * CHUNK, CHUNK), CHUNK)]
            at = pl.multiple_of(half * w_cols + n * CHUNK, CHUNK)
            g = og[:, :, pl.ds(at, CHUNK)].reshape(HW, CHUNK)
            acc_g[...] += lax.dot_general(w, g, NT, preferred_element_type=F32)
            return carry

        lax.fori_loop(0, n_inner, step, 0)

    arrived(g_half)
    arrived(g_last)
    project(dp)
    far_w.wait_recv()
    project(1 - dp)
    for h in range(G):
        dot_t[:, h * HW:(h + 1) * HW] = acc_g[h * HW:(h + 1) * HW, :].astype(BF16)

    for r in range(NZ):
        arrived(k_in[HY, r])
    over(chunks_at(HY), score)

    scale = HW ** -0.5
    top = jnp.max(mb[...], axis=0, keepdims=True) * (scale * LOG2E)

    def soften(c, carry):
        total = lb[...]
        for j in range(2 * NZ):
            rows = slice(j * BLK, (j + 1) * BLK)
            e = jnp.exp2(sb[c, rows, :] * (scale * LOG2E) - top)
            total = total + jnp.sum(e.reshape(BLK // 8, 8, QN), axis=0)
            eb[c, rows, :] = e.astype(BF16)
        lb[...] = total
        return carry

    lax.fori_loop(0, NY, soften, 0)
    inv = 1.0 / jnp.sum(lb[...], axis=0, keepdims=True)
    for h in range(G):
        cols = slice(h * HW, (h + 1) * HW)
        scaled = dot_t[:, cols].astype(F32) * inv[:, cols]
        dot_n[cols, :] = scaled.T.astype(BF16)

    def value_grad(c):
        g = dot(eb[c], dot_n[...])
        vs[...] += jnp.sum(g.reshape(ROWS // 8, 8, HW), axis=0)
        pv[c] = g.astype(BF16).reshape(NZ, HW, HW)

    def attend(c):
        acc_o[...] += lax.dot_general(whole(vb, c), eb[c], TN, preferred_element_type=F32)

    def send_terms(term, r, up, down, k):
        if up:
            term.out[k, r, 0] = wires.start(term.buf.at[HY - k, r], term.slots.at[k, 0, r], y_peer(1))
        if down:
            term.out[k, r, 1] = wires.start(term.buf.at[HY + k, r], term.slots.at[k, 1, r], y_peer(-1))

    def scatter(term, k):
        for r in range(NZ):
            for way, c in ((0, HY - k), (1, HY + k)):
                if (k - 1, r, way) in term.out:
                    term.out[k - 1, r, way].wait_recv()
                    term.buf[c, r] = (term.buf[c, r].astype(F32) + term.slots[k - 1, way, r].astype(F32)).astype(BF16)
            send_terms(term, r, k > 0 or r in lower, k > 0 or r not in lower, k)

    def settle(term):
        for r in order + [0]:
            arrived([term.out[HY - 1, r, way] for way in (0, 1)])
            both = term.slots[HY - 1, 0, r].astype(F32) + term.slots[HY - 1, 1, r].astype(F32)
            term.buf[0, r] = (term.buf[0, r].astype(F32) + both).astype(BF16)
            if r:
                term.last.append(wires.start(term.buf.at[0, r], term.landing.at[r - 1], z_peer(r)))

    def total_of(term):
        arrived(term.last)
        g = term.buf[0, 0].astype(F32)
        for r in range(NZ - 1):
            g = g + term.landing[r].astype(F32)
        return g

    def send_far(term, chunks):
        for c in chunks:
            for r in order[::-1]:
                term.first[c, r] = wires.start(term.buf.at[c, r], term.middle.at[far.index(c), r - 1], z_peer(r))

    def send_near(term, chunks):
        for c in chunks:
            term.direct.append(wires.start(term.buf.at[c], term.slots.at[near.index(c)], y_peer(c)))

    def pass_on(term):
        for c in far:
            g = term.buf[c, 0].astype(F32)
            for r in order[::-1]:
                term.first[c, r].wait_recv()
                g = g + term.middle[far.index(c), r - 1].astype(F32)
            term.buf[c, 0] = g.astype(BF16)
            term.last.append(wires.start(term.buf.at[c, 0], term.far_slots.at[far.index(c)], y_peer(c)))

    def finish_near(term):
        arrived(term.direct)
        for r in order[::-1]:
            g = term.buf[0, r].astype(F32)
            for i in range(len(near)):
                g = g + term.slots[i, r].astype(F32)
            term.buf[0, r] = g.astype(BF16)
            term.last.append(wires.start(term.buf.at[0, r], term.landing.at[r - 1], z_peer(r)))

    def whole_of(term):
        arrived(term.last)
        g = term.buf[0, 0].astype(F32)
        for i in range(len(near)):
            g = g + term.slots[i, 0].astype(F32)
        for i in range(len(far)):
            g = g + term.far_slots[i].astype(F32)
        for r in range(NZ - 1):
            g = g + term.landing[r].astype(F32)
        return g

    v_term, k_term = Direct(pv, rv, rv_f, rv_m, rv_z), Direct(pk, rk, rk_f, rk_m, rk_z)

    for n, pair in enumerate(pairs(far)):
        over(pair, value_grad)
        send_far(v_term, pair)
        if n == 0:
            forward(vb, v_in, HY - 1, order)
    for pair in pairs(near):
        over(pair, value_grad)
        send_near(v_term, pair)
    for k in range(HY):
        over(chunks_at(k), attend)
    for r in range(NZ):
        arrived(v_in[HY, r])
    over(chunks_at(HY), attend)
    o_t = (acc_o[...] * inv).astype(BF16)
    delta = jnp.sum(o_t.astype(F32) * dot_t[...].astype(F32), axis=0, keepdims=True) * inv
    for h in range(G):
        cols = slice(h * HW, (h + 1) * HW)
        o_rows[:, cols] = o_t[:, cols].astype(F32).T.astype(BF16)

    def key_grad(c):
        gp = dot(whole(vb, c), dot_t[...])
        gs = (eb[c].astype(F32) * (gp * inv - delta)).astype(BF16)
        acc_q[...] += lax.dot_general(whole(kb, c), gs, TN, preferred_element_type=F32)
        g = dot(gs, qn[...]) * scale
        pk[c] = g.astype(BF16).reshape(NZ, HW, HW)
        for j in range(2 * NZ):
            t = g[j * BLK:(j + 1) * BLK]
            back = t * cos_i - turn(t) * sin_i
            row = block_row(c, j // 2) * 2 + j % 2
            ub[pl.ds(row, 1), :] = jnp.sum(back, axis=0, keepdims=True)

    def mix(n, carry):
        half = n // n_inner
        at = pl.multiple_of(lax.rem(n, n_inner) * CHUNK, CHUNK)
        r = dot(o_rows[...], wb[half, :, pl.ds(at, CHUNK)]).astype(BF16)
        to = pl.multiple_of(n * CHUNK, CHUNK)
        po[:, :, :, pl.ds(to, CHUNK)] = r.reshape(NZL, NX, HW // (NZL * NX), CHUNK)
        return carry

    x_far, x_up, x_down = (lax.rem(x + d, NX) for d in (HX, 1, NX - 1))

    lax.fori_loop(0, 2 * n_inner, mix, 0)
    o_far = [
        wires.start(po.at[:, x_far, :, left], rx_half.at[0], x_peer(1)),
        wires.start(po.at[:, x_far, :, right], rx_half.at[1], x_peer(-1)),
    ]
    o_near = [
        wires.start(po.at[:, x_up, :, right], rx_full.at[0, :, :, right], x_peer(1)),
        wires.start(po.at[:, x_down, :, left], rx_full.at[1, :, :, left], x_peer(-1)),
    ]
    for pair in pairs(far):
        over(pair, key_grad)
        send_far(k_term, pair)
    pass_on(v_term)

    for pair in pairs(near):
        over(pair, key_grad)
        send_near(k_term, pair)
    arrived(o_far)
    po[:, x_up, :, left] = (po[:, x_up, :, left].astype(F32) + rx_half[0].astype(F32)).astype(BF16)
    po[:, x_down, :, right] = (po[:, x_down, :, right].astype(F32) + rx_half[1].astype(F32)).astype(BF16)
    o_near += [
        wires.start(po.at[:, x_up, :, left], rx_full.at[0, :, :, left], x_peer(1)),
        wires.start(po.at[:, x_down, :, right], rx_full.at[1, :, :, right], x_peer(-1)),
    ]
    over([0], key_grad)
    over([0], value_grad)
    finish_near(v_term)
    pass_on(k_term)

    for h in range(G):
        cols = slice(h * HW, (h + 1) * HW)
        g = acc_q[:, cols].T * scale
        g = g * cos - turn(g) * sin
        qg_ref[0, :, cols] = g.astype(BF16)
        btile[0, h:h + 1, :] = jnp.sum(g, axis=0, keepdims=True)
    base_angle = bpv[...].astype(F32) * freq
    u = ub[...]
    u = u * jnp.cos(base_angle) - turn(u) * (jnp.sin(base_angle) * sign)
    btile[0, G:G + 1, :] = jnp.sum(u, axis=0, keepdims=True)
    btile[0, G + 1:G + 2, :] = jnp.sum(vs[...], axis=0, keepdims=True)
    btile[0, G + 2:8, :] = jnp.zeros((8 - G - 2, HW), F32)
    bias_dp = wires.start(btile.at[0], b_dp, dp_peer)

    finish_near(k_term)

    bias_dp.wait_recv()
    btile[1] = btile[0] + b_dp[...]
    bias_z = [wires.start(btile.at[1], b_z.at[r - 1], z_peer(r)) for r in range(1, NZ)]

    arrived(o_near)
    other = 1 - zl
    zs[...] = (
        po[other, x].astype(F32) + rx_full[0, other].astype(F32) + rx_full[1, other].astype(F32)
    ).astype(BF16)
    o_z = wires.start(zs, rz, zl_peer)

    arrived(bias_z)
    total = btile[1]
    for r in range(NZ - 1):
        total = total + b_z[r]
    btile[2] = total
    bias_y = [wires.start(btile.at[2], b_y.at[d - 1], y_peer(d)) for d in range(1, NY)]

    vg_ref[0] = whole_of(v_term).astype(BF16)

    o_z.wait_recv()
    out_ref[0] = (
        po[zl, x].astype(F32)
        + rx_full[0, zl].astype(F32)
        + rx_full[1, zl].astype(F32)
        + rz[...].astype(F32)
    ).astype(BF16)

    g = whole_of(k_term)
    kg_ref[0] = (g * cos - turn(g) * sin).astype(BF16)

    arrived(bias_y)
    for d in range(NY - 1):
        total = total + b_y[d]
    bias_ref[...] = total
    wires.finish()


def layer(mesh_shape, q_in, key_input, value_input, q_bias, key_bias, value_bias, out_weight, out_grad, doc_lengths, block_pos):
    NY, NX = mesh_shape["ctx"] // NZ, mesh_shape["tp"] // NZL
    rows, features = q_in.shape[1:]
    G = features // HW
    own_rows, width = out_grad.shape[1:]
    w_cols = out_weight.shape[1]
    QN = G * HW
    ROWS = NZ * HW
    freq = ROPE_BASE ** (-np.arange(0, HW, 2, dtype=np.float64) / HW)
    freq = jnp.asarray(np.concatenate([freq, freq])[None].astype(np.float32))
    vmem, anywhere = pl.BlockSpec(memory_space=pltpu.VMEM), pl.BlockSpec(memory_space=pl.ANY)
    smem = pl.BlockSpec(memory_space=pltpu.SMEM)
    V = pltpu.VMEM
    HY = NY // 2
    ring = [V((HY, 2, NZ, HW, HW), BF16), V((NZ - 1, HW, HW), BF16)]
    near, far = (len(chunks) for chunks in near_and_far(NY))
    direct = [
        V((near, NZ, HW, HW), BF16),
        V((far, HW, HW), BF16),
        V((far, NZ - 1, HW, HW), BF16),
        V((NZ - 1, HW, HW), BF16),
    ]
    copies = 4 * (NZ - 1 + NZ * (2 * HY - 1)) + 16 + NZ + NY
    outs = pl.pallas_call(
        functools.partial(kernel, (NY, NX, G)),
        out_shape=(
            jax.ShapeDtypeStruct((1, own_rows, width), BF16),
            jax.ShapeDtypeStruct((1, rows, features), BF16),
            jax.ShapeDtypeStruct((1, rows, HW), BF16),
            jax.ShapeDtypeStruct((1, rows, HW), BF16),
            jax.ShapeDtypeStruct((8, HW), F32),
        ),
        in_specs=[vmem] * 7 + [smem] * 2 + [anywhere] * 2,
        out_specs=(vmem,) * 5,
        scratch_shapes=[
            V((QN, HW), BF16),
            V((HW, QN), BF16),
            V((NY, NZ, HW, HW), BF16),
            V((NY, NZ, HW, HW), BF16),
            V((NY, ROWS, QN), F32),
            V((NY, ROWS, QN), BF16),
            V((2, features, w_cols), BF16),
            V((NZL * NX, own_rows, width), BF16),
            V((HW, QN), BF16),
            V((QN, HW), BF16),
            V((HW, QN), BF16),
            V((HW, QN), F32),
            V((HW, QN), F32),
            V((QN, HW), F32),
            V((NY, NZ, HW, HW), BF16),
            V((NY, NZ, HW, HW), BF16),
            *direct,
            *direct,
            V((NZL, NX, own_rows, width), BF16),
            V((2, NZL, own_rows, w_cols), BF16),
            V((2, NZL, own_rows, width), BF16),
            V((own_rows, width), BF16),
            V((own_rows, width), BF16),
            V((8, QN), F32),
            V((8, QN), F32),
            V((2 * NZ * NY, HW), F32),
            V((2 * NZ * NY, HW), jnp.int32),
            V((8, HW), F32),
            V((3, 8, HW), F32),
            V((8, HW), F32),
            V((NZ - 1, 8, HW), F32),
            V((NY - 1, 8, HW), F32),
            pltpu.SemaphoreType.DMA((2,)),
            pltpu.SemaphoreType.DMA((copies,)),
            pltpu.SemaphoreType.DMA((copies,)),
        ],
        compiler_params=pltpu.CompilerParams(
            collective_id=0, has_side_effects=True, vmem_limit_bytes=60 * 1024 * 1024
        ),
        name="attention_layer",
    )(
        q_in, key_input, value_input, q_bias, key_bias.reshape(1, -1),
        value_bias.reshape(1, -1), freq, jnp.swapaxes(block_pos, 1, 2), doc_lengths, out_weight, out_grad[0],
    )
    shapes = [jax.ShapeDtypeStruct(o.shape, o.dtype) for o in outs[:4]]
    shapes += [jax.ShapeDtypeStruct((n,), F32) for n in (features, HW, HW)]
    return pl.pallas_call(
        functools.partial(finish, G),
        out_shape=tuple(shapes),
        in_specs=[vmem] * 5,
        out_specs=(vmem,) * 7,
        compiler_params=pltpu.CompilerParams(vmem_limit_bytes=60 * 1024 * 1024),
        name="hand_over",
    )(*outs)


def finish(G, *refs):
    bias_ref, biases = refs[4], refs[9:]
    for source, target in zip(refs[:4], refs[5:9]):
        target[...] = source[...]
    for h in range(G):
        biases[0][h * HW:(h + 1) * HW] = bias_ref[h]
    biases[1][...] = bias_ref[G]
    biases[2][...] = bias_ref[G + 1]


def solution(mesh):
    return jax.shard_map(
        functools.partial(layer, dict(mesh.shape)),
        mesh=mesh,
        in_specs=(
            P("dp", "ctx", "tp"),
            P("dp", "ctx", "tp"),
            P("dp", "ctx", "tp"),
            P("tp"),
            P("tp"),
            P("tp"),
            P("tp", "dp"),
            P("dp", ("ctx", "tp"), None),
            P("dp", None),
            P("dp", None, None),
        ),
        out_specs=(
            P("dp", ("ctx", "tp"), None),
            P("dp", "ctx", "tp"),
            P("dp", "ctx", "tp"),
            P("dp", "ctx", "tp"),
            P("tp"),
            P("tp"),
            P("tp"),
        ),
        check_vma=False,
    )
```
